128 devices in a mesh: snd: 16 (over x, z), cell: 8 (over y, core).
Axes of the slice: x: 4, y: 4, z: 4, core: 2. Of those that a mesh axis runs over, the one named last changes fastest.
Arguments:
- probes: bfloat16 [1024, 4, 32, 128], P(('snd', 'cell')), may hold values from -6 to 6
- spatial: bfloat16 [1024, 128, 128], P(('snd', 'cell')), may hold values from -0.5 to 0.5
- rho: float32 [1024], P(('snd', 'cell')), may hold values from 0.3 to 0.9
- foot_tile: int32 [16384, 4], P('snd'), may hold values from 0 to 1023, all different within a row; in each aligned block of 1024 rows (0 to 1023, 1024 to 2047, ...) at most 8 rows name the same one
- foot_week: int32 [16384, 4], P('snd'), may hold values from 0 to 3
- footprint: bfloat16 [16384, 4, 128], P('snd'), may hold values from 0.049804688 to 1
- sigma: float32 [16384], P('snd'), may hold values from 3 to 12
Outputs:
- probe_image: float32 [1024, 4, 32, 128], P(('snd', 'cell'))
- variance_drop: float32 [1024, 4, 128], P(('snd', 'cell'))
The draws below stay inside these ranges and needn't reach their ends.
Inputs may be any that keep to these rules, and one draw needn't show every extreme that they name: `foot_tile`: the 4 tiles of one sounding differ. In every aligned block of 1024 soundings no tile is named by more than 8 soundings, a bound that some block reaches.
All inputs are finite; a program needn't handle non-finite values.
Results may differ from the reference program's by a relative error of at most 0.0037.
Values may be sent and summed in bfloat16 or wider, within the bound.
A program may use at most 128 MiB of HBM per device.

```python
import math
import jax
import jax.numpy as jnp
import numpy as np
from jax import lax

C = 128
P_SIZE = 32
W = 4
K = 4
SND_DEV = 1024
TILES = 1024
SOUND = 16384
MOST = 8


def with_ends(values, own_key, smallest, high):
    extent = values.shape
    spot = [jax.random.randint(jax.random.fold_in(own_key, axis), (), 0, extent[axis]) for axis in range(len(extent))]
    values = values.at[tuple(spot)].set(smallest)
    longest = extent.index(max(extent))
    spot[longest] = (spot[longest] + 1) % extent[longest]
    return values.at[tuple(spot)].set(high)


def shard_levels(rng, shape, pieces, least, largest):
    level, own = 1.0, jax.random.fold_in(rng, 6)
    for position, blocks in pieces:
        draws = jnp.exp(jax.random.uniform(jax.random.fold_in(own, position), (blocks,), jnp.float32, least / len(pieces), largest / len(pieces)))
        level = level * jnp.repeat(draws, shape[position] // blocks).reshape([-1 if axis == position else 1 for axis in range(len(shape))])
    return level


def shared_out(stream_key, own, number, rows, number_of, top, bound, skew):
    sequence = jax.random.permutation(stream_key, number_of)
    crowded, usual = load_shares(number_of, rows * top, bound, skew, True), load_shares(number_of, rows * top, bound, skew, False)
    places = jnp.arange(number_of)

    def named(sizes, offset_by):
        used = int((sizes > 0).sum())
        fixed = max(1, used // 4)
        moved = fixed + (places - fixed + offset_by * (used - fixed)) % max(1, number_of - fixed)
        return jnp.zeros((number_of,), jnp.int32).at[sequence[jnp.where(places < fixed, places, moved)]].set(jnp.asarray(sizes, jnp.int32))

    sizes = jnp.where(number % 4 == 0, named(crowded, number // 4), named(usual, number - number // 4 - 1))
    mixed = jax.random.permutation(jax.random.fold_in(own, 3), number_of)
    giver, receiver = mixed[0:number_of // 2 * 2:2], mixed[1:number_of // 2 * 2:2]
    slack = jnp.minimum(sizes[giver] - 1, bound - sizes[receiver]) // 2
    slack = jnp.where((giver == sequence[0]) | (receiver == sequence[0]) | (sizes[receiver] == 0), 0, jnp.maximum(slack, 0))
    moved = jax.random.randint(jax.random.fold_in(own, 4), (number_of // 2,), 0, 1 << 20) % (slack + 1)
    sizes = sizes.at[giver].add(-moved).at[receiver].add(moved)
    labels = jnp.searchsorted(jnp.cumsum(sizes), jnp.arange(rows * top), side="right").astype(jnp.int32)
    listing = labels.reshape(top, rows).T
    listing = listing[jax.random.permutation(jax.random.fold_in(own, 1), rows)]
    offset_by = jax.random.randint(jax.random.fold_in(own, 2), (rows, 1), 0, top)
    return jnp.take_along_axis(listing, (jnp.arange(top)[None, :] + offset_by) % top, axis=1)


def load_shares(number_of, total, reach, slope, full):
    weights = [(1 << 20) // math.isqrt(grade ** slope) + 1 for grade in range(1, number_of + 1)]
    largest = reach if full else min(reach, max(-(-total // number_of), total * weights[0] // sum(weights)))
    least = 1 if total - largest >= number_of - 1 else 0
    holding, surplus = [largest] + [least] * (number_of - 1), total - largest - least * (number_of - 1)
    while surplus > 0:
        movable = [i for i in range(1, number_of) if holding[i] < largest] or [i for i in range(1, number_of) if holding[i] < reach]
        mass, left = sum([weights[i] for i in movable]), surplus
        for i in movable:
            more = min(reach - holding[i], max(1, left * weights[i] // mass), surplus)
            holding[i] = holding[i] + more
            surplus = surplus - more
    return np.array(holding)


def centred(key, dims, scale, reach, cuts=(), held_as=jnp.bfloat16):
    array = jax.random.normal(key, dims, jnp.float32) * scale
    if len(cuts) > 0:
        array = shard_levels(key, dims, cuts, -0.22, 0.18) * array
    return jnp.clip(array, min=-reach, max=reach).astype(held_as)


def setup_inputs(seed: int = 0) -> dict:
    seeds = jax.random.split(jax.random.key(seed), 8)
    probes = centred(seeds[0], (TILES, W, P_SIZE, C), 1.0, 6.0, ((0, 128),))
    spatial = centred(seeds[1], (TILES, C, C), C ** -0.5, 0.5, ((0, 128),))
    rho = jnp.clip(jnp.exp(math.log(0.9) - 1.0986122 * jax.random.uniform(seeds[2], (TILES,), jnp.float32) ** shard_levels(seeds[2], (TILES,), ((0, 128),), -0.2, 0.2)), 0.3, 0.9)
    foot_tile_keys = jax.random.split(jax.random.fold_in(seeds[3], 1), SOUND // SND_DEV)
    foot_tile_turns = jax.random.permutation(jax.random.fold_in(seeds[3], 3), SOUND // SND_DEV)
    foot_tile = jax.vmap(lambda own, number: shared_out(jax.random.fold_in(seeds[3], 2), own, number, SND_DEV, TILES, K, MOST, 2))(foot_tile_keys, foot_tile_turns).reshape((SOUND, K))
    foot_week = with_ends(jax.random.randint(seeds[4], (SOUND, K), 0, W), jax.random.fold_in(seeds[4], 1), 0, W - 1).astype(jnp.int32)
    footprint = jnp.clip(jnp.exp(math.log(1.0) - 2.9996462 * jax.random.uniform(seeds[5], (SOUND, K, C), jnp.float32) ** shard_levels(seeds[5], (SOUND, K, C), ((0, 16),), -0.2, 0.2)), 0.049804688, 1.0).astype(jnp.bfloat16)
    sigma = jnp.clip(jnp.exp(math.log(12.0) - 1.3862944 * jax.random.uniform(seeds[6], (SOUND,), jnp.float32) ** shard_levels(seeds[6], (SOUND,), ((0, 16),), -0.2, 0.2)), 3.0, 12.0)
    return dict(probes=probes, spatial=spatial, rho=rho, foot_tile=foot_tile, foot_week=foot_week, footprint=footprint, sigma=sigma)


def prior_apply(probes, spatial, rho):
    spread = jnp.einsum('twpj,tij->twpi', probes.astype(jnp.float32), spatial.astype(jnp.float32))
    running = spread[:, 0]
    stacked = [running]
    for week_step in range(1, W):
        running = spread[:, week_step] + rho[:, None, None] * running
        stacked.append(running)
    return jnp.stack(stacked, 1).astype(jnp.bfloat16)


def reference(probes, spatial, rho, foot_tile, foot_week, footprint, sigma):
    prior_field = prior_apply(probes, spatial, rho)
    lookup = prior_field.reshape(TILES * W, P_SIZE * C)
    row_ids = (foot_tile * W + foot_week).reshape(-1).astype(jnp.int32)
    entries = row_ids.shape[0]
    block_rows = min(4096, entries)
    block_count = entries // block_rows
    foot_blocks = footprint.reshape(block_count, block_rows, C)
    row_blocks = row_ids.reshape(block_count, block_rows)

    def forward(inputs):
        rowset, shapes = inputs
        fetched = lookup[rowset].reshape(block_rows, P_SIZE, C).astype(jnp.float32)
        return jnp.einsum('epc,ec->ep', fetched, shapes.astype(jnp.float32))

    seen_sums = lax.map(forward, (row_blocks, foot_blocks)).reshape(SOUND, K, P_SIZE).sum(1)
    weighted = seen_sums / (sigma * sigma)[:, None]
    entry_weights = jnp.broadcast_to(weighted[:, None, :], (SOUND, K, P_SIZE)).reshape(block_count, block_rows, P_SIZE)

    def accumulate(summed_total, inputs):
        rowset, shapes, values_here = inputs
        contrib = (shapes.astype(jnp.float32)[:, None, :] * values_here[:, :, None]).reshape(block_rows, P_SIZE * C)
        return summed_total.at[rowset].add(contrib), None

    adjoint, _ = lax.scan(accumulate, jnp.zeros((TILES * W, P_SIZE * C), jnp.float32), (row_blocks, foot_blocks, entry_weights))
    adjoint = adjoint.reshape(TILES, W, P_SIZE, C)
    running = adjoint[:, W - 1]
    stacked = [running]
    for week_step in range(W - 2, -1, -1):
        running = adjoint[:, week_step] + rho[:, None, None] * running
        stacked.append(running)
    carried = jnp.stack(stacked[::-1], 1).astype(jnp.bfloat16)
    probe_image = jnp.einsum('twpi,tij->twpj', carried.astype(jnp.float32), spatial.astype(jnp.float32))
    variance_drop = jnp.mean(probes.astype(jnp.float32) * probe_image, axis=2)
    return probe_image, variance_drop
```

```python
import functools

import jax
import jax.numpy as jnp
from jax import lax
from jax.experimental import pallas as pl
from jax.experimental.pallas import tpu as pltpu
from jax.sharding import PartitionSpec as P

BF = jnp.bfloat16
F32 = jnp.float32
MESH = pl.DeviceIdType.MESH

TT = 8
SLOTS = 64
WEEKS = 4
PROBES = 32
CELLS = 128


def dot_nn(a, b):
    return lax.dot_general(a, b, (((1,), (0,)), ((), ())), preferred_element_type=F32)


def dot_nt(a, b):
    return lax.dot_general(a, b, (((1,), (1,)), ((), ())), preferred_element_type=F32)


def iota(shape, dim):
    return lax.broadcasted_iota(jnp.int32, shape, dim)


def low_half(rows):
    return iota((rows, 128), 1) < 64


def pack(block, odd):
    low = low_half(16)
    if odd:
        return jnp.where(low, pltpu.roll(block[:16], 64, 1), block[16:])
    return jnp.where(low, block[:16], pltpu.roll(block[16:], 64, 1))


def unpack(even, odd):
    low = low_half(16)
    upper = jnp.where(low, even, pltpu.roll(odd, 64, 1))
    lower = jnp.where(low, pltpu.roll(even, 64, 1), odd)
    return jnp.concatenate([upper, lower], axis=0)


def doubled(ranks):
    rows, cols = ranks.shape
    wide = ranks.reshape(rows // 8, 8, cols)
    return jnp.concatenate([wide, wide - 1.0], axis=1).reshape(2 * rows, cols).astype(BF)


def one_hot(ranks):
    rows, cols = ranks.shape
    wide = ranks.reshape(rows // 16, 16, cols)
    one, zero = jnp.ones((), BF), jnp.zeros((), BF)
    rows_of = [jnp.where(wide == jnp.asarray(2 * q, BF), one, zero) for q in range(4)]
    return jnp.concatenate(rows_of, axis=1).reshape(4 * rows, cols)


def kernel(
    ns, nc, sound,
    probes_ref, spatial_ref, rho_ref, tile_ref, week_ref, foot_hbm, sigma_ref,
    image_ref, drop_ref,
    foot_ref, ranks_ref, hot_ref, field_ref,
    send_f, recv_f, send_k, recv_k, send_v, recv_v, send_r, recv_r, send_w, recv_w, send_p, recv_p,
    load_sem, ss_f, rs_f, ss_k, rs_k, ss_v, rs_v, ss_r, rs_r, ss_w, rs_w, ss_p, rs_p,
):
    me = lax.axis_index("snd")
    mine = lax.axis_index("cell")
    nj = ns * TT
    blocks = sound // 128
    chunk = sound // nc

    load = pltpu.make_async_copy(foot_hbm, foot_ref, load_sem)
    load.start()

    barrier = pltpu.get_barrier_semaphore()

    @pl.loop(1, ns)
    def _(d):
        pl.semaphore_signal(barrier, inc=1, device_id={"snd": (me + d) % ns, "cell": mine}, device_id_type=MESH)

    @pl.loop(1, nc)
    def _(d):
        pl.semaphore_signal(barrier, inc=1, device_id={"snd": me, "cell": (mine + d) % nc}, device_id_type=MESH)

    def to_snd(src, dst, ss, rs, dest):
        return pltpu.make_async_remote_copy(
            src_ref=src.at[dest], dst_ref=dst.at[me], send_sem=ss.at[dest], recv_sem=rs.at[me],
            device_id={"snd": dest, "cell": mine}, device_id_type=MESH,
        )

    def from_snd(src, dst, ss, rs, source):
        return pltpu.make_async_remote_copy(
            src_ref=src.at[source], dst_ref=dst.at[source], send_sem=ss.at[source], recv_sem=rs.at[source],
            device_id={"snd": source, "cell": mine}, device_id_type=MESH,
        )

    def to_cell(src, dst, ss, rs, dest):
        return pltpu.make_async_remote_copy(
            src_ref=src, dst_ref=dst.at[mine], send_sem=ss.at[dest], recv_sem=rs.at[mine],
            device_id={"snd": me, "cell": dest}, device_id_type=MESH,
        )

    def from_cell(src, dst, ss, rs, source):
        return pltpu.make_async_remote_copy(
            src_ref=src, dst_ref=dst.at[source], send_sem=ss.at[source], recv_sem=rs.at[source],
            device_id={"snd": me, "cell": source}, device_id_type=MESH,
        )

    def send_all(src, dst, ss, rs):
        dst[me] = src[me]

        @pl.loop(1, ns)
        def _(d):
            to_snd(src, dst, ss, rs, (me + d) % ns).start()

    def wait_all(src, dst, ss, rs):
        @pl.loop(1, ns)
        def _(d):
            from_snd(src, dst, ss, rs, (me + d) % ns).wait_recv()

    tiles = tile_ref[...]
    shift = nc.bit_length() - 1
    matched = ((tiles >> 3) & (nc - 1)) == mine
    local = jnp.where(matched, ((tiles >> (3 + shift)) << 3) | (tiles & 7), -1)
    weeks = week_ref[...]
    row_j = iota((nj, 256), 0)
    upper = jnp.where(iota((256, 256), 0) < iota((256, 256), 1), 1.0, 0.0).astype(BF)
    counts = jnp.concatenate([upper, jnp.ones((256, 256), BF)], axis=1)
    spread_e = jnp.where(iota((128, 512), 0) == iota((128, 512), 1) >> 2, 1.0, 0.0).astype(BF)
    pick_k = (iota((WEEKS, 512), 1) & 3) == iota((WEEKS, 512), 0)
    row_e = iota((nj, 512), 0).astype(F32)
    carry = jnp.zeros((nj, 256), F32)
    ranks_n = []
    weeks_n = []
    for b in range(sound // 256):
        lanes = slice(256 * b, 256 * b + 256)
        named = jnp.zeros((nj, 256), F32)
        week_of = jnp.zeros((nj, 256), F32)
        for k in range(4):
            same = local[k : k + 1, lanes] == row_j
            named = jnp.where(same, 1.0, named)
            week_of = jnp.where(same, weeks[k : k + 1, lanes].astype(F32), week_of)
        counted = dot_nn(named.astype(BF), counts)
        rank = jnp.where(named > 0.0, counted[:, :256] + carry, -1.0)
        carry = carry + counted[:, 256:]
        ranks_n.append(rank)
        weeks_n.append(week_of.astype(BF))
        for half in range(2):
            a = 2 * b + half
            here = slice(128 * a, 128 * a + 128)
            spread_rank = dot_nn(rank[:, 128 * half : 128 * half + 128].astype(BF), spread_e)
            spread_tile = dot_nn(local[:, here].astype(F32).astype(BF), spread_e)
            tile_e = jnp.sum(jnp.where(pick_k, spread_tile, 0.0), axis=0, keepdims=True)
            ranks_ref[a] = doubled(jnp.where(tile_e == row_e, spread_rank, -1.0))

    pl.semaphore_wait(barrier, ns - 1 + nc - 1)
    load.wait()

    groups = ns // 4
    mx, mz = me // 4, me % 4
    for g in range(groups):
        gx = (mx + 1 + g) % groups
        rows = pl.ds(pl.multiple_of(gx * 64, 64), 64)
        total = jnp.zeros((256, CELLS), F32)
        for a in range(blocks):
            total = total + dot_nn(one_hot(ranks_ref[a, rows, :]), foot_ref[512 * a : 512 * a + 512, :])
        send_f[pl.ds(pl.multiple_of(gx * 4, 4), 4)] = total.astype(BF).reshape(4, SLOTS, CELLS)
        if g < groups - 1:
            for dz in range(4):
                to_snd(send_f, recv_f, ss_f, rs_f, gx * 4 + (mz + dz) % 4).start()
        else:
            for dz in range(1, 4):
                to_snd(send_f, recv_f, ss_f, rs_f, gx * 4 + (mz + dz) % 4).start()
    recv_f[me] = send_f[me]

    for b in range(sound // 256):
        hot_ref[:, 256 * b : 256 * b + 256] = one_hot(doubled(ranks_n[b]))
    week_nj = jnp.concatenate(weeks_n, axis=1)
    half_tile = (iota((16, 128), 1) & 7) == (iota((16, 128), 0) & 7)
    half_own = (iota((16, 128), 1) < 64) == (iota((16, 128), 0) < 8)
    for b in range(ns // 2):
        found = dot_nt(week_nj[16 * b : 16 * b + 16], hot_ref[128 * b : 128 * b + 128, :])
        found = jnp.where(half_tile & half_own, found, 0.0)
        found = found + pltpu.roll(found, 64, 1)
        for odd in range(2):
            row = jnp.sum(found[8 * odd : 8 * odd + 8], axis=0, keepdims=True)
            send_k[2 * b + odd] = jnp.broadcast_to(row, (16, 128)).astype(BF)
    send_all(send_k, recv_k, ss_k, rs_k)

    for t in range(TT):
        spread = dot_nt(probes_ref[t], spatial_ref[t])
        running = spread[:PROBES]
        field_ref[t, :PROBES] = running.astype(BF)
        for w in range(1, WEEKS):
            running = spread[PROBES * w : PROBES * w + PROBES] + rho_ref[t] * running
            field_ref[t, PROBES * w : PROBES * w + PROBES] = running.astype(BF)

    wait_all(send_f, recv_f, ss_f, rs_f)
    wait_all(send_k, recv_k, ss_k, rs_k)
    lane_tile = iota((PROBES, 128), 1) & 7
    fields = field_ref[...].reshape(TT * WEEKS * PROBES, CELLS)
    codes = []
    for b in range(ns // 2):
        code = jnp.where(low_half(16), recv_k[2 * b].astype(F32), recv_k[2 * b + 1].astype(F32))
        codes.append(jnp.concatenate([code, code], axis=0))
    for b in range(ns // 2):
        full = dot_nt(fields, recv_f[2 * b : 2 * b + 2].reshape(128, CELLS))
        full = full.reshape(TT, WEEKS, PROBES, 128)
        value = jnp.zeros((PROBES, 128), F32)
        for w in range(WEEKS):
            here = full[0, w]
            for t in range(1, TT):
                here = jnp.where(lane_tile == t, full[t, w], here)
            value = jnp.where(codes[b] == float(w), here, value)
        for odd in range(2):
            send_v[2 * b + odd] = pack(value, odd).astype(BF)
    send_all(send_v, recv_v, ss_v, rs_v)
    wait_all(send_v, recv_v, ss_v, rs_v)

    values = jnp.concatenate(
        [unpack(recv_v[2 * b].astype(F32), recv_v[2 * b + 1].astype(F32)).astype(BF) for b in range(ns // 2)], axis=1
    )
    seen = dot_nn(values, hot_ref[...])
    for c in range(nc):
        send_r[c] = seen[:, chunk * c : chunk * c + chunk]

    @pl.loop(1, nc)
    def _(d):
        dest = (mine + d) % nc
        to_cell(send_r.at[dest], recv_r, ss_r, rs_r, dest).start()

    recv_r[mine] = send_r[mine]

    @pl.loop(1, nc)
    def _(d):
        source = (mine + d) % nc
        from_cell(send_r.at[source], recv_r, ss_r, rs_r, source).wait_recv()

    total = recv_r[0]
    for c in range(1, nc):
        total = total + recv_r[c]
    sigma = sigma_ref[pl.ds(mine, 1), :]
    send_w[...] = (total / (sigma * sigma)).astype(BF)

    @pl.loop(1, nc)
    def _(d):
        to_cell(send_w, recv_w, ss_w, rs_w, (mine + d) % nc).start()

    recv_w[mine] = send_w[...]

    @pl.loop(1, nc)
    def _(d):
        from_cell(send_w, recv_w, ss_w, rs_w, (mine + d) % nc).wait_recv()

    weighted = jnp.concatenate([recv_w[c] for c in range(nc)], axis=1)
    slot_values = dot_nt(weighted, hot_ref[...])
    for b in range(ns // 2):
        for odd in range(2):
            send_p[2 * b + odd] = pack(slot_values[:, 128 * b : 128 * b + 128], odd).astype(BF)
    send_all(send_p, recv_p, ss_p, rs_p)
    wait_all(send_p, recv_p, ss_p, rs_p)

    slot_weights = [unpack(recv_p[2 * b].astype(F32), recv_p[2 * b + 1].astype(F32)) for b in range(ns // 2)]
    feet = recv_f[...].reshape(ns * SLOTS, CELLS)
    for t in range(TT):
        parts = []
        for b in range(ns // 2):
            kept = jnp.where(lane_tile == t, slot_weights[b], 0.0)
            by_week = [jnp.where(codes[b] == float(w), kept, 0.0) for w in range(WEEKS)]
            parts.append(jnp.concatenate(by_week, axis=0).astype(BF))
        adjoint = dot_nn(jnp.concatenate(parts, axis=1), feet)
        running = adjoint[PROBES * (WEEKS - 1) :]
        carried = [running]
        for w in range(WEEKS - 2, -1, -1):
            running = adjoint[PROBES * w : PROBES * w + PROBES] + rho_ref[t] * running
            carried.append(running)
        image = dot_nn(jnp.concatenate(carried[::-1], axis=0).astype(BF), spatial_ref[t])
        image_ref[t] = image
        product = (probes_ref[t].astype(F32) * image).reshape(WEEKS, PROBES, CELLS)
        drop_ref[t] = jnp.sum(product, axis=1) * (1.0 / PROBES)

    @pl.loop(1, ns)
    def _(d):
        other = (me + d) % ns
        from_snd(send_f, recv_f, ss_f, rs_f, other).wait_send()
        from_snd(send_k, recv_k, ss_k, rs_k, other).wait_send()
        from_snd(send_v, recv_v, ss_v, rs_v, other).wait_send()
        from_snd(send_p, recv_p, ss_p, rs_p, other).wait_send()

    @pl.loop(1, nc)
    def _(d):
        other = (mine + d) % nc
        from_cell(send_r.at[other], recv_r, ss_r, rs_r, other).wait_send()
        from_cell(send_w, recv_w, ss_w, rs_w, other).wait_send()


def per_device(probes, spatial, rho, foot_tile, foot_week, footprint, sigma):
    ns, nc = lax.axis_size("snd"), lax.axis_size("cell")
    sound = foot_tile.shape[0]
    chunk = sound // nc
    vmem = pl.BlockSpec(memory_space=pltpu.VMEM)
    dma = lambda n: pltpu.SemaphoreType.DMA((n,))
    image, drop = pl.pallas_call(
        functools.partial(kernel, ns, nc, sound),
        out_shape=(
            jax.ShapeDtypeStruct((TT, WEEKS * PROBES, CELLS), F32),
            jax.ShapeDtypeStruct((TT, WEEKS, CELLS), F32),
        ),
        in_specs=[vmem, vmem, pl.BlockSpec(memory_space=pltpu.SMEM), vmem, vmem, pl.BlockSpec(memory_space=pl.ANY), vmem],
        out_specs=(vmem, vmem),
        scratch_shapes=[
            pltpu.VMEM((sound * 4, CELLS), BF),
            pltpu.VMEM((sound // 128, ns * 16, 512), BF),
            pltpu.VMEM((ns * SLOTS, sound), BF),
            pltpu.VMEM((TT, WEEKS * PROBES, CELLS), BF),
            pltpu.VMEM((ns, SLOTS, CELLS), BF),
            pltpu.VMEM((ns, SLOTS, CELLS), BF),
            pltpu.VMEM((ns, 16, 128), BF),
            pltpu.VMEM((ns, 16, 128), BF),
            pltpu.VMEM((ns, 16, 128), BF),
            pltpu.VMEM((ns, 16, 128), BF),
            pltpu.VMEM((nc, PROBES, chunk), F32),
            pltpu.VMEM((nc, PROBES, chunk), F32),
            pltpu.VMEM((PROBES, chunk), BF),
            pltpu.VMEM((nc, PROBES, chunk), BF),
            pltpu.VMEM((ns, 16, 128), BF),
            pltpu.VMEM((ns, 16, 128), BF),
            pltpu.SemaphoreType.DMA,
            dma(ns), dma(ns), dma(ns), dma(ns), dma(ns), dma(ns),
            dma(nc), dma(nc), dma(nc), dma(nc), dma(ns), dma(ns),
        ],
        compiler_params=pltpu.CompilerParams(
            collective_id=0, has_side_effects=True, vmem_limit_bytes=48 * 1024 * 1024
        ),
    )(
        probes.reshape(TT, WEEKS * PROBES, CELLS),
        spatial,
        rho,
        foot_tile.T,
        foot_week.T,
        footprint.reshape(sound * 4, CELLS),
        sigma.reshape(nc, chunk),
    )
    return image.reshape(TT, WEEKS, PROBES, CELLS), drop


def solution(mesh):
    placed = (
        P(("snd", "cell"), None, None, None),
        P(("snd", "cell"), None, None),
        P(("snd", "cell")),
        P("snd", None),
        P("snd", None),
        P("snd", None, None),
        P("snd"),
    )
    return jax.shard_map(
        per_device,
        mesh=mesh,
        in_specs=placed,
        out_specs=(P(("snd", "cell"), None, None, None), P(("snd", "cell"), None, None)),
        check_vma=False,
    )
```

```python
import functools

import jax
import jax.numpy as jnp
from jax import lax
from jax.experimental import pallas as pl
from jax.experimental.pallas import tpu as pltpu
from jax.sharding import PartitionSpec as P

BF = jnp.bfloat16
F32 = jnp.float32
MESH = pl.DeviceIdType.MESH

TT = 8
SLOTS = 64
WEEKS = 4
PROBES = 32
CELLS = 128


def dot_nn(a, b):
    return lax.dot_general(a, b, (((1,), (0,)), ((), ())), preferred_element_type=F32)


def dot_nt(a, b):
    return lax.dot_general(a, b, (((1,), (1,)), ((), ())), preferred_element_type=F32)


def iota(shape, dim):
    return lax.broadcasted_iota(jnp.int32, shape, dim)


def low_half(rows):
    return iota((rows, 128), 1) < 64


def packed(values):
    low = low_half(16)
    rows = []
    for lanes in (slice(0, 128), slice(128, 256)):
        upper, lower = values[:16, lanes], values[16:, lanes]
        rows.append(jnp.where(low, upper, pltpu.roll(lower, 64, 1)))
        rows.append(jnp.where(low, pltpu.roll(upper, 64, 1), lower))
    return jnp.stack(rows).astype(BF)


def unpacked(block):
    low = low_half(16)
    wide = block.astype(F32)
    cols = []
    for even, odd in ((wide[0], wide[1]), (wide[2], wide[3])):
        upper = jnp.where(low, even, pltpu.roll(odd, 64, 1))
        lower = jnp.where(low, pltpu.roll(even, 64, 1), odd)
        cols.append(jnp.concatenate([upper, lower], axis=0))
    return jnp.concatenate(cols, axis=1)


def doubled(ranks):
    rows, cols = ranks.shape
    wide = ranks.reshape(rows // 8, 8, cols)
    return jnp.concatenate([wide, wide - 1.0], axis=1).reshape(2 * rows, cols).astype(BF)


def one_hot(ranks):
    rows, cols = ranks.shape
    wide = ranks.reshape(rows // 16, 16, cols)
    one, zero = jnp.ones((), BF), jnp.zeros((), BF)
    rows_of = [jnp.where(wide == jnp.asarray(2 * q, BF), one, zero) for q in range(4)]
    return jnp.concatenate(rows_of, axis=1).reshape(4 * rows, cols)


def kernel(
    ns, nc, sound,
    probes_hbm, spatial_hbm, rho_hbm, tile_hbm, week_hbm, foot_hbm, sigma_hbm,
    image_ref, drop_ref,
    probes_ref, spatial_ref, rho_ref, tile_ref, week_ref, foot_ref, sigma_ref, ranks_ref, hot_ref, field_ref, adjoint_ref,
    send_f, recv_f, send_k, recv_k, send_v, recv_v, send_p, recv_p,
    send_c, recv_c, send_y, recv_y, recv_w,
    load_sem, ss_f, rs_f, ss_k, rs_k, ss_v, rs_v, ss_p, rs_p, ss_c, rs_c, ss_y, rs_y, ss_w, rs_w,
):
    me = lax.axis_index("snd")
    mine = lax.axis_index("cell")
    core, row_y = mine % 2, mine // 2
    nj = ns * TT
    groups = ns // 4
    ny = nc // 2
    half = sound // 2
    mx, mz = me // 4, me % 4
    near = {1: [0], 2: [0, 1], 4: [0, 1, 3, 2]}[groups]
    far = near[::-1]
    far_z = [2, 1, 3, 0]

    loads = [
        pltpu.make_async_copy(src, dst, load_sem.at[i])
        for i, (src, dst) in enumerate(
            (
                (tile_hbm, tile_ref),
                (week_hbm, week_ref),
                (foot_hbm, foot_ref),
                (spatial_hbm, spatial_ref),
                (probes_hbm, probes_ref),
                (sigma_hbm, sigma_ref),
                (rho_hbm, rho_ref),
            )
        )
    ]
    for load in loads:
        load.start()

    barrier = pltpu.get_barrier_semaphore()

    def greet(snd, cell):
        pl.semaphore_signal(barrier, inc=1, device_id={"snd": snd, "cell": cell}, device_id_type=MESH)

    def group_x(dx):
        return (mx + dx) % groups

    def partner(dx, dz):
        return group_x(dx) * 4 + (mz + dz) % 4

    for dx in far:
        for dz in far_z:
            if (dx, dz) != (0, 0):
                greet(partner(dx, dz), mine)
    for dy in range(1, ny):
        greet(me, (row_y + dy) % ny * 2 + core)
    greet(me, row_y * 2 + 1 - core)

    def over_snd(refs, there, here, other):
        src, dst, ss, rs = refs
        return pltpu.make_async_remote_copy(
            src_ref=src.at[there], dst_ref=dst.at[here], send_sem=ss.at[there], recv_sem=rs.at[here],
            device_id={"snd": other, "cell": mine}, device_id_type=MESH,
        )

    def to_snd(refs, dest):
        return over_snd(refs, dest, me, dest)

    def from_snd(refs, source):
        return over_snd(refs, source, source, source)

    of_f = (send_f, recv_f, ss_f, rs_f)
    of_k = (send_k, recv_k, ss_k, rs_k)
    of_v = (send_v, recv_v, ss_v, rs_v)
    of_p = (send_p, recv_p, ss_p, rs_p)

    def send_group(refs, dx):
        for dz in far_z:
            if (dx, dz) != (0, 0):
                to_snd(refs, partner(dx, dz)).start()
        if dx == 0:
            refs[1][me] = refs[0][me]

    def wait_group(refs, dx):
        for dz in range(4):
            if (dx, dz) != (0, 0):
                from_snd(refs, partner(dx, dz)).wait_recv()

    def group_rows(dx, size):
        return pl.ds(pl.multiple_of(group_x(dx) * 4 * size, 4 * size), 4 * size)

    def group_of(dx):
        return pl.ds(pl.multiple_of(group_x(dx) * 4, 4), 4)

    loads[0].wait()
    loads[1].wait()
    tiles = tile_ref[...]
    shift = nc.bit_length() - 1
    matched = ((tiles >> 3) & (nc - 1)) == mine
    local = jnp.where(matched, ((tiles >> (3 + shift)) << 3) | (tiles & 7), -1)
    weeks = week_ref[...]
    row_j = iota((nj, 256), 0)
    upper = jnp.where(iota((256, 256), 0) < iota((256, 256), 1), 1.0, 0.0).astype(BF)
    counts = jnp.concatenate([upper, jnp.ones((256, 256), BF)], axis=1)
    spread_e = jnp.where(iota((128, 512), 0) == iota((128, 512), 1) >> 2, 1.0, 0.0).astype(BF)
    pick_k = (iota((WEEKS, 512), 1) & 3) == iota((WEEKS, 512), 0)
    row_e = iota((nj, 512), 0).astype(F32)
    carry = jnp.zeros((nj, 256), F32)
    ranks_n = []
    weeks_n = []
    for b in range(sound // 256):
        lanes = slice(256 * b, 256 * b + 256)
        named = jnp.zeros((nj, 256), F32)
        week_of = jnp.zeros((nj, 256), F32)
        for k in range(4):
            same = local[k : k + 1, lanes] == row_j
            named = jnp.where(same, 1.0, named)
            week_of = jnp.where(same, weeks[k : k + 1, lanes].astype(F32), week_of)
        counted = dot_nn(named.astype(BF), counts)
        rank = jnp.where(named > 0.0, counted[:, :256] + carry, -1.0)
        carry = carry + counted[:, 256:]
        ranks_n.append(rank)
        weeks_n.append(week_of.astype(BF))
        for part in range(2):
            a = 2 * b + part
            here = slice(128 * a, 128 * a + 128)
            spread_rank = dot_nn(rank[:, 128 * part : 128 * part + 128].astype(BF), spread_e)
            spread_tile = dot_nn(local[:, here].astype(F32).astype(BF), spread_e)
            tile_e = jnp.sum(jnp.where(pick_k, spread_tile, 0.0), axis=0, keepdims=True)
            ranks_ref[a] = doubled(jnp.where(tile_e == row_e, spread_rank, -1.0))

    loads[2].wait()

    def pick_feet(dx):
        total = jnp.zeros((256, CELLS), F32)
        for a in range(sound // 128):
            total = total + dot_nn(one_hot(ranks_ref[a, group_rows(dx, 16), :]), foot_ref[512 * a : 512 * a + 512, :])
        send_f[group_of(dx)] = total.astype(BF).reshape(4, SLOTS, CELLS)

    for dx in far[:-1]:
        pick_feet(dx)
    if groups == 1:
        pick_feet(0)
    pl.semaphore_wait(barrier, ns - 1 + ny - 1 + 1)
    for dx in far[:-1]:
        send_group(of_f, dx)
    if groups > 1:
        pick_feet(0)
    send_group(of_f, 0)

    for b in range(sound // 256):
        hot_ref[:, 256 * b : 256 * b + 256] = one_hot(doubled(ranks_n[b]))
    week_nj = jnp.concatenate(weeks_n, axis=1)
    same_tile = (iota((16, 128), 1) & 7) == (iota((16, 128), 0) & 7)
    same_owner = (iota((16, 128), 1) < 64) == (iota((16, 128), 0) < 8)
    for b in range(ns // 2):
        found = dot_nt(week_nj[16 * b : 16 * b + 16], hot_ref[128 * b : 128 * b + 128, :])
        found = jnp.where(same_tile & same_owner, found, 0.0)
        found = found + pltpu.roll(found, 64, 1)
        for odd in range(2):
            row = jnp.sum(found[8 * odd : 8 * odd + 8], axis=0, keepdims=True)
            send_k[2 * b + odd] = jnp.broadcast_to(row, (16, 128)).astype(BF)
    for dx in far:
        send_group(of_k, dx)

    for load in loads[3:]:
        load.wait()
    for t in range(TT):
        spread = dot_nt(probes_ref[t], spatial_ref[t])
        running = spread[:PROBES]
        field_ref[t, :PROBES] = running.astype(BF)
        for w in range(1, WEEKS):
            running = spread[PROBES * w : PROBES * w + PROBES] + rho_ref[t] * running
            field_ref[t, PROBES * w : PROBES * w + PROBES] = running.astype(BF)

    lane_tile = iota((PROBES, 256), 1) & 7
    fields = field_ref[...].reshape(TT * WEEKS * PROBES, CELLS)
    codes = {}
    for dx in near:
        wait_group(of_f, dx)
        wait_group(of_k, dx)
        names = recv_k[group_of(dx)].astype(F32)
        low = low_half(16)
        code = jnp.concatenate([jnp.where(low, names[0], names[1]), jnp.where(low, names[2], names[3])], axis=1)
        codes[dx] = jnp.concatenate([code, code], axis=0)
        full = dot_nt(fields, recv_f[group_of(dx)].reshape(256, CELLS))
        full = full.reshape(TT, WEEKS, PROBES, 256)
        value = jnp.zeros((PROBES, 256), F32)
        for w in range(WEEKS):
            here = full[0, w]
            for t in range(1, TT):
                here = jnp.where(lane_tile == t, full[t, w], here)
            value = jnp.where(codes[dx] == float(w), here, value)
        send_v[group_of(dx)] = packed(value)
        send_group(of_v, dx)

    seen = jnp.zeros((PROBES, sound), F32)
    for dx in near:
        wait_group(of_v, dx)
        seen = seen + dot_nn(unpacked(recv_v[group_of(dx)]).astype(BF), hot_ref[group_rows(dx, SLOTS), :])
    send_c[0] = seen[:, :half]
    send_c[1] = seen[:, half:]
    other_core = {"snd": me, "cell": row_y * 2 + 1 - core}
    swap = pltpu.make_async_remote_copy(
        src_ref=send_c.at[1 - core], dst_ref=recv_c, send_sem=ss_c, recv_sem=rs_c,
        device_id=other_core, device_id_type=MESH,
    )
    swap.start()
    swap.wait_recv()
    total = send_c[core] + recv_c[...]
    send_y[...] = total.astype(BF)

    def over_y(dy, slot):
        return pltpu.make_async_remote_copy(
            src_ref=send_y, dst_ref=recv_y.at[slot], send_sem=ss_y.at[dy], recv_sem=rs_y.at[slot],
            device_id={"snd": me, "cell": (row_y + dy) % ny * 2 + core}, device_id_type=MESH,
        )

    steps_y = {1: [], 2: [1], 4: [2, 1, 3]}[ny]
    for dy in steps_y:
        over_y(dy, row_y).start()
    for dy in reversed(steps_y):
        over_y(dy, (row_y + dy) % ny).wait_recv()
        total = total + recv_y[(row_y + dy) % ny].astype(F32)
    own = half // 128
    sigma = jnp.concatenate([sigma_ref[pl.ds(core * own + i, 1), :] for i in range(own)], axis=1)
    recv_w[core] = (total / (sigma * sigma)).astype(BF)
    share = pltpu.make_async_remote_copy(
        src_ref=recv_w.at[core], dst_ref=recv_w.at[core], send_sem=ss_w, recv_sem=rs_w,
        device_id=other_core, device_id_type=MESH,
    )
    share.start()
    share.wait_recv()

    weighted = jnp.concatenate([recv_w[0], recv_w[1]], axis=1)
    for dx in far:
        send_p[group_of(dx)] = packed(dot_nt(weighted, hot_ref[group_rows(dx, SLOTS), :]))
        send_group(of_p, dx)

    for step, dx in enumerate(near):
        wait_group(of_p, dx)
        value = unpacked(recv_p[group_of(dx)])
        by_week = [jnp.where(codes[dx] == float(w), value, 0.0) for w in range(WEEKS)]
        spread = [jnp.where(lane_tile == t, by_week[w], 0.0).astype(BF) for t in range(TT) for w in range(WEEKS)]
        part = dot_nn(jnp.concatenate(spread, axis=0), recv_f[group_of(dx)].reshape(256, CELLS))
        if step == 0:
            adjoint_ref[...] = part
        else:
            adjoint_ref[...] += part
    for t in range(TT):
        rows = WEEKS * PROBES * t
        running = adjoint_ref[rows + PROBES * (WEEKS - 1) : rows + PROBES * WEEKS, :]
        carried = [running]
        for w in range(WEEKS - 2, -1, -1):
            running = adjoint_ref[rows + PROBES * w : rows + PROBES * w + PROBES, :] + rho_ref[t] * running
            carried.append(running)
        image = dot_nn(jnp.concatenate(carried[::-1], axis=0).astype(BF), spatial_ref[t])
        image_ref[t] = image
        product = (probes_ref[t].astype(F32) * image).reshape(WEEKS, PROBES, CELLS)
        drop_ref[t] = jnp.sum(product, axis=1) * (1.0 / PROBES)

    for refs in (of_f, of_k, of_v, of_p):
        for dx in far:
            for dz in far_z:
                if (dx, dz) != (0, 0):
                    to_snd(refs, partner(dx, dz)).wait_send()
    swap.wait_send()
    share.wait_send()
    for dy in steps_y:
        over_y(dy, row_y).wait_send()


def per_device(probes, spatial, rho, foot_tile, foot_week, footprint, sigma):
    ns, nc = lax.axis_size("snd"), lax.axis_size("cell")
    sound = foot_tile.shape[0]
    half = sound // 2
    hbm = pl.BlockSpec(memory_space=pltpu.HBM)
    vmem = pl.BlockSpec(memory_space=pltpu.VMEM)
    one = pltpu.SemaphoreType.DMA
    dma = lambda n: pltpu.SemaphoreType.DMA((n,))
    operands = (
        probes.reshape(TT, WEEKS * PROBES, CELLS),
        spatial,
        rho,
        foot_tile.T,
        foot_week.T,
        footprint.reshape(sound * 4, CELLS),
        sigma.reshape(sound // 128, 128),
    )
    image, drop = pl.pallas_call(
        functools.partial(kernel, ns, nc, sound),
        out_shape=(
            jax.ShapeDtypeStruct((TT, WEEKS * PROBES, CELLS), F32),
            jax.ShapeDtypeStruct((TT, WEEKS, CELLS), F32),
        ),
        in_specs=[hbm] * 7,
        out_specs=(vmem, vmem),
        scratch_shapes=[
            pltpu.VMEM((TT, WEEKS * PROBES, CELLS), BF),
            pltpu.VMEM((TT, CELLS, CELLS), BF),
            pltpu.SMEM((TT,), F32),
            pltpu.VMEM((4, sound), jnp.int32),
            pltpu.VMEM((4, sound), jnp.int32),
            pltpu.VMEM((sound * 4, CELLS), BF),
            pltpu.VMEM((sound // 128, 128), F32),
            pltpu.VMEM((sound // 128, ns * 16, 512), BF),
            pltpu.VMEM((ns * SLOTS, sound), BF),
            pltpu.VMEM((TT, WEEKS * PROBES, CELLS), BF),
            pltpu.VMEM((TT * WEEKS * PROBES, CELLS), F32),
            pltpu.VMEM((ns, SLOTS, CELLS), BF),
            pltpu.VMEM((ns, SLOTS, CELLS), BF),
            pltpu.VMEM((ns, 16, 128), BF),
            pltpu.VMEM((ns, 16, 128), BF),
            pltpu.VMEM((ns, 16, 128), BF),
            pltpu.VMEM((ns, 16, 128), BF),
            pltpu.VMEM((ns, 16, 128), BF),
            pltpu.VMEM((ns, 16, 128), BF),
            pltpu.VMEM((2, PROBES, half), F32),
            pltpu.VMEM((PROBES, half), F32),
            pltpu.VMEM((PROBES, half), BF),
            pltpu.VMEM((nc // 2, PROBES, half), BF),
            pltpu.VMEM((2, PROBES, half), BF),
            dma(7),
            dma(ns), dma(ns), dma(ns), dma(ns), dma(ns), dma(ns), dma(ns), dma(ns),
            one, one, dma(max(2, nc // 2)), dma(nc // 2), one, one,
        ],
        compiler_params=pltpu.CompilerParams(
            collective_id=0, has_side_effects=True, vmem_limit_bytes=40 * 1024 * 1024
        ),
    )(*(pltpu.with_memory_space_constraint(x, pltpu.HBM) for x in operands))
    return image.reshape(TT, WEEKS, PROBES, CELLS), drop


def solution(mesh):
    placed = (
        P(("snd", "cell"), None, None, None),
        P(("snd", "cell"), None, None),
        P(("snd", "cell")),
        P("snd", None),
        P("snd", None),
        P("snd", None, None),
        P("snd"),
    )
    return jax.shard_map(
        per_device,
        mesh=mesh,
        in_specs=placed,
        out_specs=(P(("snd", "cell"), None, None, None), P(("snd", "cell"), None, None)),
        check_vma=False,
    )
```

```python
import functools

import jax
import jax.numpy as jnp
from jax import lax
from jax.experimental import pallas as pl
from jax.experimental.pallas import tpu as pltpu
from jax.sharding import PartitionSpec as P

BF = jnp.bfloat16
F32 = jnp.float32
MESH = pl.DeviceIdType.MESH

TT = 8
SLOTS = 64
WEEKS = 4
PROBES = 32
CELLS = 128


def dot_nn(a, b):
    return lax.dot_general(a, b, (((1,), (0,)), ((), ())), preferred_element_type=F32)


def dot_nt(a, b):
    return lax.dot_general(a, b, (((1,), (1,)), ((), ())), preferred_element_type=F32)


def iota(shape, dim):
    return lax.broadcasted_iota(jnp.int32, shape, dim)


def low_half(rows):
    return iota((rows, 128), 1) < 64


def packed(values):
    low = low_half(16)
    rows = []
    for lanes in (slice(0, 128), slice(128, 256)):
        upper, lower = values[:16, lanes], values[16:, lanes]
        rows.append(jnp.where(low, upper, pltpu.roll(lower, 64, 1)))
        rows.append(jnp.where(low, pltpu.roll(upper, 64, 1), lower))
    return jnp.stack(rows).astype(BF)


def unpacked(block):
    low = low_half(16)
    wide = block.astype(F32)
    cols = []
    for even, odd in ((wide[0], wide[1]), (wide[2], wide[3])):
        upper = jnp.where(low, even, pltpu.roll(odd, 64, 1))
        lower = jnp.where(low, pltpu.roll(even, 64, 1), odd)
        cols.append(jnp.concatenate([upper, lower], axis=0))
    return jnp.concatenate(cols, axis=1)


def doubled(ranks):
    rows, cols = ranks.shape
    wide = ranks.reshape(rows // 8, 8, cols)
    return jnp.concatenate([wide, wide - 1.0], axis=1).reshape(2 * rows, cols).astype(BF)


def one_hot(ranks):
    rows, cols = ranks.shape
    wide = ranks.reshape(rows // 16, 16, cols)
    one, zero = jnp.ones((), BF), jnp.zeros((), BF)
    rows_of = [jnp.where(wide == jnp.asarray(2 * q, BF), one, zero) for q in range(4)]
    return jnp.concatenate(rows_of, axis=1).reshape(4 * rows, cols)


def kernel(
    ns, nc, sound,
    probes_hbm, spatial_hbm, rho_hbm, tile_hbm, week_hbm, foot_hbm, sigma_hbm,
    carried_ref,
    probes_ref, spatial_ref, rho_ref, tile_ref, week_ref, foot_ref, sigma_ref, order_ref, ranks_ref, hot_ref, field_ref, adjoint_ref,
    send_f, recv_f, send_v, recv_v, send_p, recv_p,
    send_c, recv_c, send_y, recv_y, recv_w,
    load_sem, ss_f, rs_f, ss_v, rs_v, ss_p, rs_p, ss_c, rs_c, ss_y, rs_y, ss_w, rs_w,
):
    me = lax.axis_index("snd")
    mine = lax.axis_index("cell")
    core, row_y = mine % 2, mine // 2
    nj = ns * TT
    groups = ns // 4
    ny = nc // 2
    half = sound // 2
    mx, mz = me // 4, me % 4
    near = {1: [0], 2: [0, 1], 4: [0, 1, 3, 2]}[groups]
    far = near[::-1]
    far_z = [2, 1, 3, 0]

    loads = [
        pltpu.make_async_copy(src, dst, load_sem.at[i])
        for i, (src, dst) in enumerate(
            (
                (tile_hbm, tile_ref),
                (week_hbm, week_ref),
                (foot_hbm, foot_ref),
                (spatial_hbm, spatial_ref),
                (probes_hbm, probes_ref),
                (sigma_hbm, sigma_ref),
                (rho_hbm, rho_ref),
            )
        )
    ]
    for load in loads:
        load.start()

    barrier = pltpu.get_barrier_semaphore()

    def greet(snd, cell):
        pl.semaphore_signal(barrier, inc=1, device_id={"snd": snd, "cell": cell}, device_id_type=MESH)

    def group_x(dx):
        return (mx + dx) % groups

    def partner(dx, dz):
        return group_x(dx) * 4 + (mz + dz) % 4

    for dx in far:
        for dz in far_z:
            if (dx, dz) != (0, 0):
                greet(partner(dx, dz), mine)
    for dy in range(1, ny):
        greet(me, (row_y + dy) % ny * 2 + core)
    greet(me, row_y * 2 + 1 - core)

    def over_snd(refs, there, here, other):
        src, dst, ss, rs = refs
        return pltpu.make_async_remote_copy(
            src_ref=src.at[there], dst_ref=dst.at[here], send_sem=ss.at[there], recv_sem=rs.at[here],
            device_id={"snd": other, "cell": mine}, device_id_type=MESH,
        )

    def to_snd(refs, dest):
        return over_snd(refs, dest, me, dest)

    def from_snd(refs, source):
        return over_snd(refs, source, source, source)

    of_f = (send_f, recv_f, ss_f, rs_f)
    of_v = (send_v, recv_v, ss_v, rs_v)
    of_p = (send_p, recv_p, ss_p, rs_p)

    def send_group(refs, dx):
        for dz in far_z:
            if (dx, dz) != (0, 0):
                to_snd(refs, partner(dx, dz)).start()
        if dx == 0:
            refs[1][me] = refs[0][me]

    def wait_group(refs, dx):
        for dz in range(4):
            if (dx, dz) != (0, 0):
                from_snd(refs, partner(dx, dz)).wait_recv()

    def group_rows(dx, size):
        return pl.ds(pl.multiple_of(group_x(dx) * 4 * size, 4 * size), 4 * size)

    def group_of(dx):
        return pl.ds(pl.multiple_of(group_x(dx) * 4, 4), 4)

    loads[0].wait()
    loads[1].wait()
    tiles = tile_ref[...]
    weeks = week_ref[...]
    shift = nc.bit_length() - 1
    row_j = iota((nj, 256), 0)
    upper = jnp.where(iota((256, 256), 0) < iota((256, 256), 1), 1.0, 0.0).astype(BF)
    counts = jnp.concatenate([upper, jnp.ones((256, 256), BF)], axis=1)
    spread_e = jnp.where(iota((128, 512), 0) == iota((128, 512), 1) >> 2, 1.0, 0.0).astype(BF)
    pick_k = (iota((WEEKS, 512), 1) & 3) == iota((WEEKS, 512), 0)
    row_e = iota((nj, 512), 0).astype(F32)

    matched = ((tiles >> 3) & (nc - 1)) == mine
    local = jnp.where(matched, ((tiles >> (3 + shift)) << 3) | (tiles & 7), -1)
    carry = jnp.zeros((nj, 256), F32)
    bits = jnp.zeros((nj, 256), F32)
    for b in range(sound // 256):
        lanes = slice(256 * b, 256 * b + 256)
        named = jnp.zeros((nj, 256), F32)
        week_of = jnp.zeros((nj, 256), jnp.int32)
        for k in range(4):
            same = local[k : k + 1, lanes] == row_j
            named = jnp.where(same, 1.0, named)
            week_of = jnp.where(same, weeks[k : k + 1, lanes], week_of)
        counted = dot_nn(named.astype(BF), counts)
        place = counted[:, :256] + carry
        order = jnp.where(named > 0.0, place, -1.0)
        carry = carry + counted[:, 256:]
        bits = bits + (week_of << (place.astype(jnp.int32) * 2)).astype(F32)
        order_ref[:, lanes] = order
        for part in range(2):
            a = 2 * b + part
            here = slice(128 * a, 128 * a + 128)
            spread_rank = dot_nn(order[:, 128 * part : 128 * part + 128].astype(BF), spread_e)
            spread_tile = dot_nn(local[:, here].astype(F32).astype(BF), spread_e)
            tile_e = jnp.sum(jnp.where(pick_k, spread_tile, 0.0), axis=0, keepdims=True)
            ranks_ref[a] = doubled(jnp.where(tile_e == row_e, spread_rank, -1.0))

    bits = jnp.sum(bits, axis=1, keepdims=True).astype(jnp.int32)
    lane = iota((TT, 128), 1)
    for d in range(ns):
        word = jnp.broadcast_to(bits[TT * d : TT * d + TT], (TT, 128))
        week = (word >> (((lane & 63) >> 3) * 2)) & 3
        row = jnp.sum(jnp.where((lane & 7) == iota((TT, 128), 0), week.astype(F32), 0.0), axis=0, keepdims=True)
        send_f[d, SLOTS:] = jnp.broadcast_to(row, (16, 128)).astype(BF)

    loads[2].wait()

    def pick_feet(dx):
        total = jnp.zeros((256, CELLS), F32)
        for a in range(sound // 128):
            total = total + dot_nn(one_hot(ranks_ref[a, group_rows(dx, 16), :]), foot_ref[512 * a : 512 * a + 512, :])
        send_f[group_of(dx), :SLOTS] = total.astype(BF).reshape(4, SLOTS, CELLS)

    for dx in far[:-1]:
        pick_feet(dx)
    if groups == 1:
        pick_feet(0)
    pl.semaphore_wait(barrier, ns - 1 + ny - 1 + 1)
    for dx in far[:-1]:
        send_group(of_f, dx)
    if groups > 1:
        pick_feet(0)
    send_group(of_f, 0)

    for b in range(sound // 256):
        lanes = slice(256 * b, 256 * b + 256)
        hot_ref[:, lanes] = one_hot(doubled(order_ref[:, lanes]))

    for load in loads[3:]:
        load.wait()
    for t in range(TT):
        spread = dot_nt(probes_ref[t], spatial_ref[t])
        running = spread[:PROBES]
        field_ref[t, :PROBES] = running.astype(BF)
        for w in range(1, WEEKS):
            running = spread[PROBES * w : PROBES * w + PROBES] + rho_ref[t] * running
            field_ref[t, PROBES * w : PROBES * w + PROBES] = running.astype(BF)

    lane_tile = iota((PROBES, 256), 1) & 7
    fields = field_ref[...].reshape(TT * WEEKS * PROBES, CELLS)
    codes = {}
    for dx in near:
        wait_group(of_f, dx)
        names = recv_f[group_of(dx), SLOTS:].astype(F32)
        low = low_half(16)
        code = jnp.concatenate([jnp.where(low, names[0], names[1]), jnp.where(low, names[2], names[3])], axis=1)
        codes[dx] = jnp.concatenate([code, code], axis=0)
        full = dot_nt(fields, recv_f[group_of(dx), :SLOTS].reshape(256, CELLS))
        full = full.reshape(TT, WEEKS, PROBES, 256)
        value = jnp.zeros((PROBES, 256), F32)
        for w in range(WEEKS):
            here = full[0, w]
            for t in range(1, TT):
                here = jnp.where(lane_tile == t, full[t, w], here)
            value = jnp.where(codes[dx] == float(w), here, value)
        send_v[group_of(dx)] = packed(value)
        send_group(of_v, dx)

    seen = jnp.zeros((PROBES, sound), F32)
    for dx in near:
        wait_group(of_v, dx)
        seen = seen + dot_nn(unpacked(recv_v[group_of(dx)]).astype(BF), hot_ref[group_rows(dx, SLOTS), :])
    send_c[0] = seen[:, :half]
    send_c[1] = seen[:, half:]
    other_core = {"snd": me, "cell": row_y * 2 + 1 - core}
    swap = pltpu.make_async_remote_copy(
        src_ref=send_c.at[1 - core], dst_ref=recv_c, send_sem=ss_c, recv_sem=rs_c,
        device_id=other_core, device_id_type=MESH,
    )
    swap.start()
    swap.wait_recv()
    total = send_c[core] + recv_c[...]
    send_y[...] = total.astype(BF)

    def over_y(dy, slot):
        return pltpu.make_async_remote_copy(
            src_ref=send_y, dst_ref=recv_y.at[slot], send_sem=ss_y.at[dy], recv_sem=rs_y.at[slot],
            device_id={"snd": me, "cell": (row_y + dy) % ny * 2 + core}, device_id_type=MESH,
        )

    steps_y = {1: [], 2: [1], 4: [2, 1, 3]}[ny]
    for dy in steps_y:
        over_y(dy, row_y).start()
    for dy in reversed(steps_y):
        over_y(dy, (row_y + dy) % ny).wait_recv()
        total = total + recv_y[(row_y + dy) % ny].astype(F32)
    own = half // 128
    sigma = jnp.concatenate([sigma_ref[pl.ds(core * own + i, 1), :] for i in range(own)], axis=1)
    recv_w[core] = (total / (sigma * sigma)).astype(BF)
    share = pltpu.make_async_remote_copy(
        src_ref=recv_w.at[core], dst_ref=recv_w.at[core], send_sem=ss_w, recv_sem=rs_w,
        device_id=other_core, device_id_type=MESH,
    )
    share.start()
    share.wait_recv()

    weighted = jnp.concatenate([recv_w[0], recv_w[1]], axis=1)
    for dx in far:
        send_p[group_of(dx)] = packed(dot_nt(weighted, hot_ref[group_rows(dx, SLOTS), :]))
        send_group(of_p, dx)

    for step, dx in enumerate(near):
        wait_group(of_p, dx)
        value = unpacked(recv_p[group_of(dx)])
        by_week = [jnp.where(codes[dx] == float(w), value, 0.0) for w in range(WEEKS)]
        spread = [jnp.where(lane_tile == t, by_week[w], 0.0).astype(BF) for t in range(TT) for w in range(WEEKS)]
        adjoint = dot_nn(jnp.concatenate(spread, axis=0), recv_f[group_of(dx), :SLOTS].reshape(256, CELLS))
        if step > 0:
            adjoint = adjoint + adjoint_ref[...]
        if step < groups - 1:
            adjoint_ref[...] = adjoint
    for t in range(TT):
        rows = WEEKS * PROBES * t
        running = adjoint[rows + PROBES * (WEEKS - 1) : rows + PROBES * WEEKS]
        carried = [running]
        for w in range(WEEKS - 2, -1, -1):
            running = adjoint[rows + PROBES * w : rows + PROBES * w + PROBES] + rho_ref[t] * running
            carried.append(running)
        carried_ref[t] = jnp.concatenate(carried[::-1], axis=0).astype(BF)

    for refs in (of_f, of_v, of_p):
        for dx in far:
            for dz in far_z:
                if (dx, dz) != (0, 0):
                    to_snd(refs, partner(dx, dz)).wait_send()
    swap.wait_send()
    share.wait_send()
    for dy in steps_y:
        over_y(dy, row_y).wait_send()


def finish(carried_ref, spatial_ref, probes_ref, image_hbm, drop_hbm, image_ref, drop_ref, sems):
    stores = [pltpu.make_async_copy(image_ref.at[t], image_hbm.at[t], sems.at[t]) for t in range(TT)]
    for t in range(TT):
        image = dot_nn(carried_ref[t], spatial_ref[t])
        image_ref[t] = image
        stores[t].start()
        product = (probes_ref[t].astype(F32) * image).reshape(WEEKS, PROBES, CELLS)
        drop_ref[t] = jnp.sum(product, axis=1) * (1.0 / PROBES)
    last = pltpu.make_async_copy(drop_ref, drop_hbm, sems.at[TT])
    last.start()
    for store in stores:
        store.wait()
    last.wait()


def per_device(probes, spatial, rho, foot_tile, foot_week, footprint, sigma):
    ns, nc = lax.axis_size("snd"), lax.axis_size("cell")
    sound = foot_tile.shape[0]
    half = sound // 2
    hbm = pl.BlockSpec(memory_space=pltpu.HBM)
    vmem = pl.BlockSpec(memory_space=pltpu.VMEM)
    one = pltpu.SemaphoreType.DMA
    dma = lambda n: pltpu.SemaphoreType.DMA((n,))
    operands = (
        probes.reshape(TT, WEEKS * PROBES, CELLS),
        spatial,
        rho,
        foot_tile.T,
        foot_week.T,
        footprint.reshape(sound * 4, CELLS),
        sigma.reshape(sound // 128, 128),
    )
    carried = pl.pallas_call(
        functools.partial(kernel, ns, nc, sound),
        out_shape=jax.ShapeDtypeStruct((TT, WEEKS * PROBES, CELLS), BF),
        in_specs=[hbm] * 7,
        out_specs=vmem,
        scratch_shapes=[
            pltpu.VMEM((TT, WEEKS * PROBES, CELLS), BF),
            pltpu.VMEM((TT, CELLS, CELLS), BF),
            pltpu.SMEM((TT,), F32),
            pltpu.VMEM((4, sound), jnp.int32),
            pltpu.VMEM((4, sound), jnp.int32),
            pltpu.VMEM((sound * 4, CELLS), BF),
            pltpu.VMEM((sound // 128, 128), F32),
            pltpu.VMEM((ns * TT, sound), F32),
            pltpu.VMEM((sound // 128, ns * 16, 512), BF),
            pltpu.VMEM((ns * SLOTS, sound), BF),
            pltpu.VMEM((TT, WEEKS * PROBES, CELLS), BF),
            pltpu.VMEM((TT * WEEKS * PROBES, CELLS), F32),
            pltpu.VMEM((ns, SLOTS + 16, CELLS), BF),
            pltpu.VMEM((ns, SLOTS + 16, CELLS), BF),
            pltpu.VMEM((ns, 16, 128), BF),
            pltpu.VMEM((ns, 16, 128), BF),
            pltpu.VMEM((ns, 16, 128), BF),
            pltpu.VMEM((ns, 16, 128), BF),
            pltpu.VMEM((2, PROBES, half), F32),
            pltpu.VMEM((PROBES, half), F32),
            pltpu.VMEM((PROBES, half), BF),
            pltpu.VMEM((nc // 2, PROBES, half), BF),
            pltpu.VMEM((2, PROBES, half), BF),
            dma(7),
            dma(ns), dma(ns), dma(ns), dma(ns), dma(ns), dma(ns),
            one, one, dma(max(2, nc // 2)), dma(nc // 2), one, one,
        ],
        compiler_params=pltpu.CompilerParams(
            collective_id=0, has_side_effects=True, vmem_limit_bytes=40 * 1024 * 1024
        ),
    )(*(pltpu.with_memory_space_constraint(x, pltpu.HBM) for x in operands))
    image, drop = pl.pallas_call(
        finish,
        out_shape=(
            jax.ShapeDtypeStruct((TT, WEEKS * PROBES, CELLS), F32),
            jax.ShapeDtypeStruct((TT, WEEKS, CELLS), F32),
        ),
        in_specs=[vmem] * 3,
        out_specs=(hbm, hbm),
        scratch_shapes=[
            pltpu.VMEM((TT, WEEKS * PROBES, CELLS), F32),
            pltpu.VMEM((TT, WEEKS, CELLS), F32),
            dma(TT + 1),
        ],
        compiler_params=pltpu.CompilerParams(vmem_limit_bytes=4 * 1024 * 1024),
    )(carried, spatial, probes.reshape(TT, WEEKS * PROBES, CELLS))
    return image.reshape(TT, WEEKS, PROBES, CELLS), drop


def solution(mesh):
    placed = (
        P(("snd", "cell"), None, None, None),
        P(("snd", "cell"), None, None),
        P(("snd", "cell")),
        P("snd", None),
        P("snd", None),
        P("snd", None, None),
        P("snd"),
    )
    return jax.shard_map(
        per_device,
        mesh=mesh,
        in_specs=placed,
        out_specs=(P(("snd", "cell"), None, None, None), P(("snd", "cell"), None, None)),
        check_vma=False,
    )
```

```python
import functools

import jax
import jax.numpy as jnp
from jax import lax
from jax.experimental import pallas as pl
from jax.experimental.pallas import tpu as pltpu
from jax.sharding import PartitionSpec as P

BF = jnp.bfloat16
F32 = jnp.float32
MESH = pl.DeviceIdType.MESH

TT = 8
SLOTS = 64
WEEKS = 4
PROBES = 32
CELLS = 128


def dot_nn(a, b):
    return lax.dot_general(a, b, (((1,), (0,)), ((), ())), preferred_element_type=F32)


def dot_nt(a, b):
    return lax.dot_general(a, b, (((1,), (1,)), ((), ())), preferred_element_type=F32)


def iota(shape, dim):
    return lax.broadcasted_iota(jnp.int32, shape, dim)


def low_half(rows):
    return iota((rows, 128), 1) < 64


def packed(values):
    low = low_half(16)
    rows = []
    for lanes in (slice(0, 128), slice(128, 256)):
        upper, lower = values[:16, lanes], values[16:, lanes]
        rows.append(jnp.where(low, upper, pltpu.roll(lower, 64, 1)))
        rows.append(jnp.where(low, pltpu.roll(upper, 64, 1), lower))
    return jnp.stack(rows).astype(BF)


def unpacked(block):
    low = low_half(16)
    wide = block.astype(F32)
    cols = []
    for even, odd in ((wide[0], wide[1]), (wide[2], wide[3])):
        upper = jnp.where(low, even, pltpu.roll(odd, 64, 1))
        lower = jnp.where(low, pltpu.roll(even, 64, 1), odd)
        cols.append(jnp.concatenate([upper, lower], axis=0))
    return jnp.concatenate(cols, axis=1)


def doubled(ranks):
    rows, cols = ranks.shape
    wide = ranks.reshape(rows // 8, 8, cols)
    return jnp.concatenate([wide, wide - 1.0], axis=1).reshape(2 * rows, cols).astype(BF)


def one_hot(*ranks):
    rows, cols = ranks[0].shape
    wide = [r.reshape(rows // 16, 16, cols) for r in ranks]
    one, zero = jnp.ones((), BF), jnp.zeros((), BF)
    rows_of = []
    for q in range(4):
        same = wide[0] == jnp.asarray(2 * q, BF)
        for r in wide[1:]:
            same = same | (r == jnp.asarray(2 * q, BF))
        rows_of.append(jnp.where(same, one, zero))
    return jnp.concatenate(rows_of, axis=1).reshape(4 * rows, cols)


def kernel(
    ns, nc, sound,
    probes_hbm, spatial_hbm, rho_hbm, tile_hbm, week_hbm, foot_hbm, sigma_hbm,
    carried_ref,
    probes_ref, spatial_ref, rho_ref, tile_ref, week_ref, foot_ref, sigma_ref, order_ref, early_ref, ranks_ref, hot_ref, field_ref,
    send_f, recv_f, send_v, recv_v, send_p, recv_p,
    send_c, recv_c, send_y, recv_y, recv_w,
    load_sem, ss_f, rs_f, ss_v, rs_v, ss_p, rs_p, ss_c, rs_c, ss_y, rs_y, ss_w, rs_w,
):
    me = lax.axis_index("snd")
    mine = lax.axis_index("cell")
    core, row_y = mine % 2, mine // 2
    nj = ns * TT
    groups = ns // 4
    ny = nc // 2
    half = sound // 2
    mx, mz = me // 4, me % 4
    near = {1: [0], 2: [0, 1], 4: [0, 1, 3, 2]}[groups]
    far = near[::-1]
    far_z = [2, 1, 3, 0]

    loads = [
        pltpu.make_async_copy(src, dst, load_sem.at[i])
        for i, (src, dst) in enumerate(
            (
                (tile_hbm, tile_ref),
                (week_hbm, week_ref),
                (foot_hbm, foot_ref),
                (spatial_hbm, spatial_ref),
                (probes_hbm, probes_ref),
                (sigma_hbm, sigma_ref),
                (rho_hbm, rho_ref),
            )
        )
    ]
    for load in loads:
        load.start()

    barrier = pltpu.get_barrier_semaphore()

    def greet(snd, cell):
        pl.semaphore_signal(barrier, inc=1, device_id={"snd": snd, "cell": cell}, device_id_type=MESH)

    def group_x(dx):
        return (mx + dx) % groups

    def partner(dx, dz):
        return group_x(dx) * 4 + (mz + dz) % 4

    for dx in far:
        for dz in far_z:
            if (dx, dz) != (0, 0):
                greet(partner(dx, dz), mine)
    for dy in range(1, ny):
        greet(me, (row_y + dy) % ny * 2 + core)
    greet(me, row_y * 2 + 1 - core)

    def over_snd(refs, there, here, other):
        src, dst, ss, rs = refs
        return pltpu.make_async_remote_copy(
            src_ref=src.at[there], dst_ref=dst.at[here], send_sem=ss.at[there], recv_sem=rs.at[here],
            device_id={"snd": other, "cell": mine}, device_id_type=MESH,
        )

    def to_snd(refs, dest):
        return over_snd(refs, dest, me, dest)

    def from_snd(refs, source):
        return over_snd(refs, source, source, source)

    of_f = (send_f, recv_f, ss_f, rs_f)
    of_v = (send_v, recv_v, ss_v, rs_v)
    of_p = (send_p, recv_p, ss_p, rs_p)

    def send_group(refs, dx):
        for dz in far_z:
            if (dx, dz) != (0, 0):
                to_snd(refs, partner(dx, dz)).start()
        if dx == 0:
            refs[1][me] = refs[0][me]

    def wait_group(refs, dx):
        for dz in range(4):
            if (dx, dz) != (0, 0):
                from_snd(refs, partner(dx, dz)).wait_recv()

    def sent(refs):
        for dx in far:
            for dz in far_z:
                if (dx, dz) != (0, 0):
                    to_snd(refs, partner(dx, dz)).wait_send()

    def group_rows(dx, size):
        return pl.ds(pl.multiple_of(group_x(dx) * 4 * size, 4 * size), 4 * size)

    def group_of(dx):
        return pl.ds(pl.multiple_of(group_x(dx) * 4, 4), 4)

    loads[0].wait()
    loads[1].wait()
    tiles = tile_ref[...]
    weeks = week_ref[...]
    shift = nc.bit_length() - 1
    width = min(256, sound // 2)
    row_j = iota((nj, width), 0)
    upper = jnp.where(iota((width, width), 0) < iota((width, width), 1), 1.0, 0.0).astype(BF)
    counts = jnp.concatenate([upper, jnp.ones((width, width), BF)], axis=1)
    spread_e = jnp.where(iota((128, 512), 0) == iota((128, 512), 1) >> 2, 1.0, 0.0).astype(BF)
    pick_k = (iota((WEEKS, 512), 1) & 3) == iota((WEEKS, 512), 0)
    row_e = iota((nj, 512), 0).astype(F32)

    matched = ((tiles >> 3) & (nc - 1)) == mine
    local = jnp.where(matched, ((tiles >> (3 + shift)) << 3) | (tiles & 7), -1)
    carry = jnp.zeros((nj, width), F32)
    bits = jnp.zeros((nj, width), F32)
    for b in range(sound // width):
        if 2 * width * b == sound:
            early_ref[...] = carry[:, :128]
        lanes = slice(width * b, width * b + width)
        named = jnp.zeros((nj, width), F32)
        week_of = jnp.zeros((nj, width), jnp.int32)
        for k in range(4):
            same = local[k : k + 1, lanes] == row_j
            named = jnp.where(same, 1.0, named)
            week_of = jnp.where(same, weeks[k : k + 1, lanes], week_of)
        counted = dot_nn(named.astype(BF), counts)
        place = counted[:, :width] + carry
        order = jnp.where(named > 0.0, place, -1.0)
        carry = carry + counted[:, width:]
        bits = bits + (week_of << (place.astype(jnp.int32) * 2)).astype(F32)
        order_ref[:, lanes] = order
        for part in range(width // 128):
            a = width // 128 * b + part
            here = slice(128 * a, 128 * a + 128)
            spread_rank = dot_nn(order[:, 128 * part : 128 * part + 128].astype(BF), spread_e)
            spread_tile = dot_nn(local[:, here].astype(F32).astype(BF), spread_e)
            tile_e = jnp.sum(jnp.where(pick_k, spread_tile, 0.0), axis=0, keepdims=True)
            ranks_ref[a] = doubled(jnp.where(tile_e == row_e, spread_rank, -1.0))

    bits = jnp.sum(bits, axis=1, keepdims=True).astype(jnp.int32)
    lane = iota((TT, 128), 1)
    for d in range(ns):
        word = jnp.broadcast_to(bits[TT * d : TT * d + TT], (TT, 128))
        week = (word >> (((lane & 63) >> 3) * 2)) & 3
        row = jnp.sum(jnp.where((lane & 7) == iota((TT, 128), 0), week.astype(F32), 0.0), axis=0, keepdims=True)
        send_f[d, SLOTS:] = jnp.broadcast_to(row, (16, 128)).astype(BF)

    loads[2].wait()

    both = jnp.concatenate([foot_ref[: 2 * sound, :], foot_ref[2 * sound :, :]], axis=1)
    pairs = sound // 256

    def pick_feet(dx):
        for part in range(2):
            first = group_x(dx) * 4 + 2 * part
            rows = pl.ds(pl.multiple_of(first * 16, 32), 32)
            picks = [one_hot(ranks_ref[a, rows, :], ranks_ref[a + pairs, rows, :]) for a in range(pairs)]
            found = dot_nn(jnp.concatenate(picks, axis=1), both).reshape(2, 8, TT, 2 * CELLS)
            early = early_ref[pl.ds(pl.multiple_of(first * TT, 16), 16), :].reshape(2, TT, CELLS)
            kept = [jnp.where(early > float(r), found[:, r, :, :CELLS], found[:, r, :, CELLS:]) for r in range(8)]
            send_f[pl.ds(first, 2), :SLOTS] = jnp.stack(kept, axis=1).reshape(2, SLOTS, CELLS).astype(BF)

    for dx in far[:-1]:
        pick_feet(dx)
    if groups == 1:
        pick_feet(0)
    pl.semaphore_wait(barrier, ns - 1 + ny - 1 + 1)
    for dx in far[:-1]:
        send_group(of_f, dx)
    if groups > 1:
        pick_feet(0)
    send_group(of_f, 0)

    for b in range(sound // 256):
        lanes = slice(256 * b, 256 * b + 256)
        hot_ref[:, lanes] = one_hot(doubled(order_ref[:, lanes]))

    for load in loads[3:]:
        load.wait()
    for t in range(TT):
        spread = dot_nt(probes_ref[t], spatial_ref[t])
        running = spread[:PROBES]
        field_ref[t, :PROBES] = running.astype(BF)
        for w in range(1, WEEKS):
            running = spread[PROBES * w : PROBES * w + PROBES] + rho_ref[t] * running
            field_ref[t, PROBES * w : PROBES * w + PROBES] = running.astype(BF)

    lane_tile = iota((PROBES, 256), 1) & 7
    fields = field_ref[...].reshape(TT * WEEKS * PROBES, CELLS)
    codes = {}
    for dx in near:
        wait_group(of_f, dx)
    for dx in near:
        names = recv_f[group_of(dx), SLOTS:].astype(F32)
        low = low_half(16)
        code = jnp.concatenate([jnp.where(low, names[0], names[1]), jnp.where(low, names[2], names[3])], axis=1)
        codes[dx] = jnp.concatenate([code, code], axis=0)
        full = dot_nt(fields, recv_f[group_of(dx), :SLOTS].reshape(256, CELLS))
        full = full.reshape(TT, WEEKS, PROBES, 256)
        value = jnp.zeros((PROBES, 256), F32)
        for w in range(WEEKS):
            here = full[0, w]
            for t in range(1, TT):
                here = jnp.where(lane_tile == t, full[t, w], here)
            value = jnp.where(codes[dx] == float(w), here, value)
        send_v[group_of(dx)] = packed(value)
    for dx in far:
        send_group(of_v, dx)

    sent(of_f)

    seen = jnp.zeros((PROBES, sound), F32)
    for dx in near:
        wait_group(of_v, dx)
    for dx in near:
        seen = seen + dot_nn(unpacked(recv_v[group_of(dx)]).astype(BF), hot_ref[group_rows(dx, SLOTS), :])
    send_c[0] = seen[:, :half]
    send_c[1] = seen[:, half:]
    other_core = {"snd": me, "cell": row_y * 2 + 1 - core}
    swap = pltpu.make_async_remote_copy(
        src_ref=send_c.at[1 - core], dst_ref=recv_c, send_sem=ss_c, recv_sem=rs_c,
        device_id=other_core, device_id_type=MESH,
    )
    swap.start()
    swap.wait_recv()
    total = send_c[core] + recv_c[...]
    send_y[...] = total.astype(BF)

    def over_y(dy, slot):
        return pltpu.make_async_remote_copy(
            src_ref=send_y, dst_ref=recv_y.at[slot], send_sem=ss_y.at[dy], recv_sem=rs_y.at[slot],
            device_id={"snd": me, "cell": (row_y + dy) % ny * 2 + core}, device_id_type=MESH,
        )

    steps_y = {1: [], 2: [1], 4: [2, 1, 3]}[ny]
    for dy in steps_y:
        over_y(dy, row_y).start()
    sent(of_v)
    swap.wait_send()
    for dy in reversed(steps_y):
        over_y(dy, (row_y + dy) % ny).wait_recv()
    for dy in reversed(steps_y):
        total = total + recv_y[(row_y + dy) % ny].astype(F32)
    own = half // 128
    sigma = jnp.concatenate([sigma_ref[pl.ds(core * own + i, 1), :] for i in range(own)], axis=1)
    recv_w[core] = (total / (sigma * sigma)).astype(BF)
    share = pltpu.make_async_remote_copy(
        src_ref=recv_w.at[core], dst_ref=recv_w.at[core], send_sem=ss_w, recv_sem=rs_w,
        device_id=other_core, device_id_type=MESH,
    )
    share.start()
    share.wait_recv()

    weighted = jnp.concatenate([recv_w[0], recv_w[1]], axis=1)
    backs = dot_nt(weighted, hot_ref[...])
    for x in range(groups):
        send_p[4 * x : 4 * x + 4] = packed(backs[:, 256 * x : 256 * x + 256])
    for dx in far:
        send_group(of_p, dx)

    for dy in steps_y:
        over_y(dy, row_y).wait_send()

    at_tile = [lane_tile.astype(F32).astype(BF) == jnp.asarray(t, BF) for t in range(TT)]
    by_week = []
    for dx in near:
        wait_group(of_p, dx)
        value, code = unpacked(recv_p[group_of(dx)]).astype(BF), codes[dx].astype(BF)
        by_week.append([jnp.where(code == jnp.asarray(w, BF), value, jnp.zeros((), BF)) for w in range(WEEKS)])
    feet = jnp.concatenate([recv_f[group_of(dx), :SLOTS].reshape(256, CELLS) for dx in near], axis=0)
    for t in range(TT):
        spread = [jnp.concatenate([jnp.where(at_tile[t], part, jnp.zeros((), BF)) for part in weeks_of], axis=0) for weeks_of in by_week]
        adjoint = dot_nn(jnp.concatenate(spread, axis=1), feet)
        running = adjoint[PROBES * (WEEKS - 1) :]
        carried = [running]
        for w in range(WEEKS - 2, -1, -1):
            running = adjoint[PROBES * w : PROBES * w + PROBES] + rho_ref[t] * running
            carried.append(running)
        carried_ref[t] = jnp.concatenate(carried[::-1], axis=0).astype(BF)

    sent(of_p)
    share.wait_send()


def finish(carried_ref, spatial_ref, probes_ref, image_hbm, drop_hbm, image_ref, drop_ref, sems):
    stores = [pltpu.make_async_copy(image_ref.at[t], image_hbm.at[t], sems.at[t]) for t in range(TT)]
    for t in range(TT):
        image = dot_nn(carried_ref[t], spatial_ref[t])
        image_ref[t] = image
        stores[t].start()
        product = (probes_ref[t].astype(F32) * image).reshape(WEEKS, PROBES, CELLS)
        drop_ref[t] = jnp.sum(product, axis=1) * (1.0 / PROBES)
    last = pltpu.make_async_copy(drop_ref, drop_hbm, sems.at[TT])
    last.start()
    for store in stores:
        store.wait()
    last.wait()


def per_device(probes, spatial, rho, foot_tile, foot_week, footprint, sigma):
    ns, nc = lax.axis_size("snd"), lax.axis_size("cell")
    sound = foot_tile.shape[0]
    half = sound // 2
    hbm = pl.BlockSpec(memory_space=pltpu.HBM)
    vmem = pl.BlockSpec(memory_space=pltpu.VMEM)
    one = pltpu.SemaphoreType.DMA
    dma = lambda n: pltpu.SemaphoreType.DMA((n,))
    operands = (
        probes.reshape(TT, WEEKS * PROBES, CELLS),
        spatial,
        rho,
        foot_tile.T,
        foot_week.T,
        footprint.reshape(sound * 4, CELLS),
        sigma.reshape(sound // 128, 128),
    )
    carried = pl.pallas_call(
        functools.partial(kernel, ns, nc, sound),
        out_shape=jax.ShapeDtypeStruct((TT, WEEKS * PROBES, CELLS), BF),
        in_specs=[hbm] * 7,
        out_specs=vmem,
        scratch_shapes=[
            pltpu.VMEM((TT, WEEKS * PROBES, CELLS), BF),
            pltpu.VMEM((TT, CELLS, CELLS), BF),
            pltpu.SMEM((TT,), F32),
            pltpu.VMEM((4, sound), jnp.int32),
            pltpu.VMEM((4, sound), jnp.int32),
            pltpu.VMEM((sound * 4, CELLS), BF),
            pltpu.VMEM((sound // 128, 128), F32),
            pltpu.VMEM((ns * TT, sound), F32),
            pltpu.VMEM((ns * TT, 128), F32),
            pltpu.VMEM((sound // 128, ns * 16, 512), BF),
            pltpu.VMEM((ns * SLOTS, sound), BF),
            pltpu.VMEM((TT, WEEKS * PROBES, CELLS), BF),
            pltpu.VMEM((ns, SLOTS + 16, CELLS), BF),
            pltpu.VMEM((ns, SLOTS + 16, CELLS), BF),
            pltpu.VMEM((ns, 16, 128), BF),
            pltpu.VMEM((ns, 16, 128), BF),
            pltpu.VMEM((ns, 16, 128), BF),
            pltpu.VMEM((ns, 16, 128), BF),
            pltpu.VMEM((2, PROBES, half), F32),
            pltpu.VMEM((PROBES, half), F32),
            pltpu.VMEM((PROBES, half), BF),
            pltpu.VMEM((nc // 2, PROBES, half), BF),
            pltpu.VMEM((2, PROBES, half), BF),
            dma(7),
            dma(ns), dma(ns), dma(ns), dma(ns), dma(ns), dma(ns),
            one, one, dma(max(2, nc // 2)), dma(nc // 2), one, one,
        ],
        compiler_params=pltpu.CompilerParams(
            collective_id=0, has_side_effects=True, vmem_limit_bytes=40 * 1024 * 1024
        ),
    )(*(pltpu.with_memory_space_constraint(x, pltpu.HBM) for x in operands))
    image, drop = pl.pallas_call(
        finish,
        out_shape=(
            jax.ShapeDtypeStruct((TT, WEEKS * PROBES, CELLS), F32),
            jax.ShapeDtypeStruct((TT, WEEKS, CELLS), F32),
        ),
        in_specs=[vmem] * 3,
        out_specs=(hbm, hbm),
        scratch_shapes=[
            pltpu.VMEM((TT, WEEKS * PROBES, CELLS), F32),
            pltpu.VMEM((TT, WEEKS, CELLS), F32),
            dma(TT + 1),
        ],
        compiler_params=pltpu.CompilerParams(vmem_limit_bytes=4 * 1024 * 1024),
    )(carried, spatial, probes.reshape(TT, WEEKS * PROBES, CELLS))
    return image.reshape(TT, WEEKS, PROBES, CELLS), drop


def solution(mesh):
    placed = (
        P(("snd", "cell"), None, None, None),
        P(("snd", "cell"), None, None),
        P(("snd", "cell")),
        P("snd", None),
        P("snd", None),
        P("snd", None, None),
        P("snd"),
    )
    return jax.shard_map(
        per_device,
        mesh=mesh,
        in_specs=placed,
        out_specs=(P(("snd", "cell"), None, None, None), P(("snd", "cell"), None, None)),
        check_vma=False,
    )
```

```python
import functools

import jax
import jax.numpy as jnp
from jax import lax
from jax.experimental import pallas as pl
from jax.experimental.pallas import tpu as pltpu
from jax.sharding import PartitionSpec as P

BF = jnp.bfloat16
F32 = jnp.float32
MESH = pl.DeviceIdType.MESH

TT = 8
SLOTS = 64
WEEKS = 4
PROBES = 32
CELLS = 128
SIDE = 2


def dot_nn(a, b):
    return lax.dot_general(a, b, (((1,), (0,)), ((), ())), preferred_element_type=F32)


def dot_nt(a, b):
    return lax.dot_general(a, b, (((1,), (1,)), ((), ())), preferred_element_type=F32)


def iota(shape, dim):
    return lax.broadcasted_iota(jnp.int32, shape, dim)


def low_half(rows):
    return iota((rows, 128), 1) < 64


def packed(values):
    low = low_half(16)
    rows = []
    for lanes in (slice(0, 128), slice(128, 256)):
        upper, lower = values[:16, lanes], values[16:, lanes]
        rows.append(jnp.where(low, upper, pltpu.roll(lower, 64, 1)))
        rows.append(jnp.where(low, pltpu.roll(upper, 64, 1), lower))
    return jnp.stack(rows).astype(BF)


def unpacked(block):
    low = low_half(16)
    wide = block.astype(F32)
    cols = []
    for even, odd in ((wide[0], wide[1]), (wide[2], wide[3])):
        upper = jnp.where(low, even, pltpu.roll(odd, 64, 1))
        lower = jnp.where(low, pltpu.roll(even, 64, 1), odd)
        cols.append(jnp.concatenate([upper, lower], axis=0))
    return jnp.concatenate(cols, axis=1)


def doubled(ranks):
    rows, cols = ranks.shape
    wide = ranks.reshape(rows // 8, 8, cols)
    return jnp.concatenate([wide, wide - 1.0], axis=1).reshape(2 * rows, cols).astype(BF)


def one_hot(*ranks):
    rows, cols = ranks[0].shape
    wide = [r.reshape(rows // 16, 16, cols) for r in ranks]
    one, zero = jnp.ones((), BF), jnp.zeros((), BF)
    rows_of = []
    for q in range(4):
        same = wide[0] == jnp.asarray(2 * q, BF)
        for r in wide[1:]:
            same = same | (r == jnp.asarray(2 * q, BF))
        rows_of.append(jnp.where(same, one, zero))
    return jnp.concatenate(rows_of, axis=1).reshape(4 * rows, cols)


def kernel(
    ns, nc, sound,
    probes_hbm, spatial_hbm, rho_hbm, tile_hbm, week_hbm, foot_hbm, sigma_hbm,
    carried_ref,
    probes_ref, spatial_ref, rho_ref, tile_ref, week_ref, foot_ref, sigma_ref, order_ref, early_ref, ranks_ref, hot_ref, field_ref, wide_ref,
    send_f, recv_f, send_v, recv_v, send_p, recv_p,
    send_c, recv_c, send_y, recv_y, recv_w,
    load_sem, ss_f, rs_f, ss_v, rs_v, ss_p, rs_p, ss_c, rs_c, ss_y, rs_y, ss_w, rs_w,
):
    me = lax.axis_index("snd")
    mine = lax.axis_index("cell")
    core, row_y = mine % 2, mine // 2
    nj = ns * TT
    groups = ns // 4
    ny = nc // 2
    half = sound // 2
    mx, mz = me // 4, me % 4
    near = {1: [0], 2: [0, 1], 4: [0, 1, 3, 2]}[groups]
    far = near[::-1]
    far_z = [2, 1, 3, 0]

    loads = [
        pltpu.make_async_copy(src, dst, load_sem.at[i])
        for i, (src, dst) in enumerate(
            (
                (tile_hbm, tile_ref),
                (week_hbm, week_ref),
                (foot_hbm, foot_ref),
                (spatial_hbm, spatial_ref),
                (probes_hbm, probes_ref),
                (sigma_hbm, sigma_ref),
                (rho_hbm, rho_ref),
            )
        )
    ]
    for load in loads:
        load.start()

    barrier = pltpu.get_barrier_semaphore()

    def greet(snd, cell):
        pl.semaphore_signal(barrier, inc=1, device_id={"snd": snd, "cell": cell}, device_id_type=MESH)

    def group_x(dx):
        return (mx + dx) % groups

    def partner(dx, dz):
        return group_x(dx) * 4 + (mz + dz) % 4

    for dx in far:
        for dz in far_z:
            if (dx, dz) != (0, 0):
                greet(partner(dx, dz), mine)
    for dy in range(1, ny):
        greet(me, (row_y + dy) % ny * 2 + core)
    greet(me, row_y * 2 + 1 - core)

    def to_snd(refs, dest):
        src, dst, ss, rs = refs
        return pltpu.make_async_remote_copy(
            src_ref=src.at[dest], dst_ref=dst.at[me], send_sem=ss, recv_sem=rs,
            device_id={"snd": dest, "cell": mine}, device_id_type=MESH,
        )

    of_f = (send_f, recv_f, ss_f, rs_f)
    of_v = (send_v, recv_v, ss_v, rs_v)
    of_p = (send_p, recv_p, ss_p, rs_p)

    def send_group(refs, dx):
        for dz in far_z:
            if (dx, dz) != (0, 0):
                to_snd(refs, partner(dx, dz)).start()
        if dx == 0:
            refs[1][me] = refs[0][me]

    def of_others(buffer, sem):
        pltpu.make_async_copy(buffer.at[pl.ds(0, ns - 1)], buffer.at[pl.ds(0, ns - 1)], sem).wait()

    def arrived(refs):
        of_others(refs[1], refs[3])

    def sent(refs):
        of_others(refs[0], refs[2])

    def group_rows(dx, size):
        return pl.ds(pl.multiple_of(group_x(dx) * 4 * size, 4 * size), 4 * size)

    def group_of(dx):
        return pl.ds(pl.multiple_of(group_x(dx) * 4, 4), 4)

    loads[0].wait()
    loads[1].wait()
    tiles = tile_ref[...]
    weeks = week_ref[...]
    shift = nc.bit_length() - 1
    width = min(256, sound // 2)
    row_j = iota((nj, width), 0)
    upper = jnp.where(iota((width, width), 0) < iota((width, width), 1), 1.0, 0.0).astype(BF)
    counts = jnp.concatenate([upper, jnp.ones((width, width), BF)], axis=1)
    spread_e = jnp.where(iota((128, 512), 0) == iota((128, 512), 1) >> 2, 1.0, 0.0).astype(BF)
    pick_k = (iota((WEEKS, 512), 1) & 3) == iota((WEEKS, 512), 0)
    row_e = iota((nj, 512), 0).astype(F32)

    matched = ((tiles >> 3) & (nc - 1)) == mine
    local = jnp.where(matched, ((tiles >> (3 + shift)) << 3) | (tiles & 7), -1)
    carry = jnp.zeros((nj, width), F32)
    bits = jnp.zeros((nj, width), F32)
    for b in range(sound // width):
        if 2 * width * b == sound:
            early_ref[...] = carry[:, :128]
        lanes = slice(width * b, width * b + width)
        named = jnp.zeros((nj, width), F32)
        week_of = jnp.zeros((nj, width), jnp.int32)
        for k in range(4):
            same = local[k : k + 1, lanes] == row_j
            named = jnp.where(same, 1.0, named)
            week_of = jnp.where(same, weeks[k : k + 1, lanes], week_of)
        counted = dot_nn(named.astype(BF), counts)
        place = counted[:, :width] + carry
        order = jnp.where(named > 0.0, place, -1.0)
        carry = carry + counted[:, width:]
        bits = bits + (week_of << (place.astype(jnp.int32) * 2)).astype(F32)
        order_ref[:, lanes] = order
        for part in range(width // 128):
            a = width // 128 * b + part
            here = slice(128 * a, 128 * a + 128)
            spread_rank = dot_nn(order[:, 128 * part : 128 * part + 128].astype(BF), spread_e)
            spread_tile = dot_nn(local[:, here].astype(F32).astype(BF), spread_e)
            tile_e = jnp.sum(jnp.where(pick_k, spread_tile, 0.0), axis=0, keepdims=True)
            ranks_ref[a] = doubled(jnp.where(tile_e == row_e, spread_rank, -1.0))

    bits = jnp.sum(bits, axis=1, keepdims=True).astype(jnp.int32)
    lane = iota((TT, 128), 1)
    for d in range(ns):
        word = jnp.broadcast_to(bits[TT * d : TT * d + TT], (TT, 128))
        week = (word >> (((lane & 63) >> 3) * 2)) & 3
        row = jnp.sum(jnp.where((lane & 7) == iota((TT, 128), 0), week.astype(F32), 0.0), axis=0, keepdims=True)
        send_f[d, SLOTS:] = jnp.broadcast_to(row, (16, 128)).astype(BF)

    loads[2].wait()

    both = jnp.concatenate([foot_ref[: 2 * sound, :], foot_ref[2 * sound :, :]], axis=1)
    pairs = sound // 256

    def pick_feet(dx):
        for part in range(2):
            first = group_x(dx) * 4 + 2 * part
            rows = pl.ds(pl.multiple_of(first * 16, 32), 32)
            picks = [one_hot(ranks_ref[a, rows, :], ranks_ref[a + pairs, rows, :]) for a in range(pairs)]
            found = dot_nn(jnp.concatenate(picks, axis=1), both).reshape(2, 8, TT, 2 * CELLS)
            early = early_ref[pl.ds(pl.multiple_of(first * TT, 16), 16), :].reshape(2, TT, CELLS)
            kept = [jnp.where(early > float(r), found[:, r, :, :CELLS], found[:, r, :, CELLS:]) for r in range(8)]
            send_f[pl.ds(first, 2), :SLOTS] = jnp.stack(kept, axis=1).reshape(2, SLOTS, CELLS).astype(BF)

    for dx in far[:-1]:
        pick_feet(dx)
    if groups == 1:
        pick_feet(0)
    pl.semaphore_wait(barrier, ns - 1 + ny - 1 + 1)
    for dx in far[:-1]:
        send_group(of_f, dx)
    if groups > 1:
        pick_feet(0)
    send_group(of_f, 0)

    for b in range(sound // 256):
        lanes = slice(256 * b, 256 * b + 256)
        hot_ref[:, lanes] = one_hot(doubled(order_ref[:, lanes]))

    for load in loads[3:]:
        load.wait()
    for t in range(TT):
        spread = dot_nt(probes_ref[t], spatial_ref[t])
        lanes = slice(CELLS * (t % SIDE), CELLS * (t % SIDE) + CELLS)
        running = spread[:PROBES]
        field_ref[t // SIDE, :PROBES, lanes] = running.astype(BF)
        for w in range(1, WEEKS):
            running = spread[PROBES * w : PROBES * w + PROBES] + rho_ref[t] * running
            field_ref[t // SIDE, PROBES * w : PROBES * w + PROBES, lanes] = running.astype(BF)

    lane_side = (iota((PROBES, 256), 1) & 7) // SIDE
    row_tile = (iota((256, CELLS), 0) & (SIDE - 1)).astype(F32).astype(BF)
    fields = field_ref[...].reshape(TT // SIDE * WEEKS * PROBES, SIDE * CELLS)
    codes = {}
    arrived(of_f)
    for dx in near:
        names = recv_f[group_of(dx), SLOTS:].astype(F32)
        low = low_half(16)
        code = jnp.concatenate([jnp.where(low, names[0], names[1]), jnp.where(low, names[2], names[3])], axis=1)
        codes[dx] = jnp.concatenate([code, code], axis=0)
        feet = recv_f[group_of(dx), :SLOTS].reshape(256, CELLS)
        sides = [jnp.where(row_tile == jnp.asarray(h, BF), feet, jnp.zeros((), BF)) for h in range(SIDE)]
        wide = jnp.concatenate(sides, axis=1)
        wide_ref[group_rows(dx, SLOTS), :] = wide
        full = dot_nt(fields, wide)
        full = full.reshape(TT // SIDE, WEEKS, PROBES, 256)
        value = jnp.zeros((PROBES, 256), F32)
        for w in range(WEEKS):
            here = full[0, w]
            for g in range(1, TT // SIDE):
                here = jnp.where(lane_side == g, full[g, w], here)
            value = jnp.where(codes[dx] == float(w), here, value)
        send_v[group_of(dx)] = packed(value)
    for dx in far:
        send_group(of_v, dx)

    sent(of_f)

    seen = jnp.zeros((PROBES, sound), F32)
    arrived(of_v)
    for dx in near:
        seen = seen + dot_nn(unpacked(recv_v[group_of(dx)]).astype(BF), hot_ref[group_rows(dx, SLOTS), :])
    send_c[0] = seen[:, :half]
    send_c[1] = seen[:, half:]
    other_core = {"snd": me, "cell": row_y * 2 + 1 - core}
    swap = pltpu.make_async_remote_copy(
        src_ref=send_c.at[1 - core], dst_ref=recv_c, send_sem=ss_c, recv_sem=rs_c,
        device_id=other_core, device_id_type=MESH,
    )
    swap.start()
    swap.wait_recv()
    total = send_c[core] + recv_c[...]
    send_y[...] = total.astype(BF)

    def over_y(dy, slot):
        return pltpu.make_async_remote_copy(
            src_ref=send_y, dst_ref=recv_y.at[slot], send_sem=ss_y.at[dy], recv_sem=rs_y.at[slot],
            device_id={"snd": me, "cell": (row_y + dy) % ny * 2 + core}, device_id_type=MESH,
        )

    steps_y = {1: [], 2: [1], 4: [2, 1, 3]}[ny]
    for dy in steps_y:
        over_y(dy, row_y).start()
    sent(of_v)
    swap.wait_send()
    for dy in reversed(steps_y):
        over_y(dy, (row_y + dy) % ny).wait_recv()
    for dy in reversed(steps_y):
        total = total + recv_y[(row_y + dy) % ny].astype(F32)
    own = half // 128
    sigma = jnp.concatenate([sigma_ref[pl.ds(core * own + i, 1), :] for i in range(own)], axis=1)
    recv_w[core] = (total / (sigma * sigma)).astype(BF)
    share = pltpu.make_async_remote_copy(
        src_ref=recv_w.at[core], dst_ref=recv_w.at[core], send_sem=ss_w, recv_sem=rs_w,
        device_id=other_core, device_id_type=MESH,
    )
    share.start()
    share.wait_recv()

    weighted = jnp.concatenate([recv_w[0], recv_w[1]], axis=1)
    backs = dot_nt(weighted, hot_ref[...])
    for x in range(groups):
        send_p[4 * x : 4 * x + 4] = packed(backs[:, 256 * x : 256 * x + 256])
    for dx in far:
        send_group(of_p, dx)

    for dy in steps_y:
        over_y(dy, row_y).wait_send()

    at_side = [lane_side.astype(F32).astype(BF) == jnp.asarray(g, BF) for g in range(TT // SIDE)]
    arrived(of_p)
    spread = []
    for dx in near:
        value, code = unpacked(recv_p[group_of(dx)]).astype(BF), codes[dx].astype(BF)
        by_week = [jnp.where(code == jnp.asarray(w, BF), value, jnp.zeros((), BF)) for w in range(WEEKS)]
        spread.append([[jnp.where(at, part, jnp.zeros((), BF)) for part in by_week] for at in at_side])
    feet = jnp.concatenate([wide_ref[group_rows(dx, SLOTS), :] for dx in near], axis=0)
    for g in range(TT // SIDE):
        kept = jnp.concatenate([jnp.concatenate(parts[g], axis=0) for parts in spread], axis=1)
        adjoint = dot_nn(kept, feet)
        for h in range(SIDE):
            here = adjoint[:, CELLS * h : CELLS * h + CELLS]
            running = here[PROBES * (WEEKS - 1) :]
            carried = [running]
            for w in range(WEEKS - 2, -1, -1):
                running = here[PROBES * w : PROBES * w + PROBES] + rho_ref[SIDE * g + h] * running
                carried.append(running)
            carried_ref[SIDE * g + h] = jnp.concatenate(carried[::-1], axis=0).astype(BF)

    sent(of_p)
    share.wait_send()


def finish(carried_ref, spatial_ref, probes_ref, image_hbm, drop_hbm, image_ref, drop_ref, sems):
    stores = [pltpu.make_async_copy(image_ref.at[t], image_hbm.at[t], sems.at[t]) for t in range(TT)]
    for t in range(TT):
        image = dot_nn(carried_ref[t], spatial_ref[t])
        image_ref[t] = image
        stores[t].start()
        product = (probes_ref[t].astype(F32) * image).reshape(WEEKS, PROBES, CELLS)
        drop_ref[t] = jnp.sum(product, axis=1) * (1.0 / PROBES)
    last = pltpu.make_async_copy(drop_ref, drop_hbm, sems.at[TT])
    last.start()
    for store in stores:
        store.wait()
    last.wait()


def per_device(probes, spatial, rho, foot_tile, foot_week, footprint, sigma):
    ns, nc = lax.axis_size("snd"), lax.axis_size("cell")
    sound = foot_tile.shape[0]
    half = sound // 2
    hbm = pl.BlockSpec(memory_space=pltpu.HBM)
    vmem = pl.BlockSpec(memory_space=pltpu.VMEM)
    one = pltpu.SemaphoreType.DMA
    dma = lambda n: pltpu.SemaphoreType.DMA((n,))
    operands = (
        probes.reshape(TT, WEEKS * PROBES, CELLS),
        spatial,
        rho,
        foot_tile.T,
        foot_week.T,
        footprint.reshape(sound * 4, CELLS),
        sigma.reshape(sound // 128, 128),
    )
    carried = pl.pallas_call(
        functools.partial(kernel, ns, nc, sound),
        out_shape=jax.ShapeDtypeStruct((TT, WEEKS * PROBES, CELLS), BF),
        in_specs=[hbm] * 7,
        out_specs=vmem,
        scratch_shapes=[
            pltpu.VMEM((TT, WEEKS * PROBES, CELLS), BF),
            pltpu.VMEM((TT, CELLS, CELLS), BF),
            pltpu.SMEM((TT,), F32),
            pltpu.VMEM((4, sound), jnp.int32),
            pltpu.VMEM((4, sound), jnp.int32),
            pltpu.VMEM((sound * 4, CELLS), BF),
            pltpu.VMEM((sound // 128, 128), F32),
            pltpu.VMEM((ns * TT, sound), F32),
            pltpu.VMEM((ns * TT, 128), F32),
            pltpu.VMEM((sound // 128, ns * 16, 512), BF),
            pltpu.VMEM((ns * SLOTS, sound), BF),
            pltpu.VMEM((TT // SIDE, WEEKS * PROBES, SIDE * CELLS), BF),
            pltpu.VMEM((ns * SLOTS, SIDE * CELLS), BF),
            pltpu.VMEM((ns, SLOTS + 16, CELLS), BF),
            pltpu.VMEM((ns, SLOTS + 16, CELLS), BF),
            pltpu.VMEM((ns, 16, 128), BF),
            pltpu.VMEM((ns, 16, 128), BF),
            pltpu.VMEM((ns, 16, 128), BF),
            pltpu.VMEM((ns, 16, 128), BF),
            pltpu.VMEM((2, PROBES, half), F32),
            pltpu.VMEM((PROBES, half), F32),
            pltpu.VMEM((PROBES, half), BF),
            pltpu.VMEM((nc // 2, PROBES, half), BF),
            pltpu.VMEM((2, PROBES, half), BF),
            dma(7),
            one, one, one, one, one, one,
            one, one, dma(max(2, nc // 2)), dma(nc // 2), one, one,
        ],
        compiler_params=pltpu.CompilerParams(
            collective_id=0, has_side_effects=True, vmem_limit_bytes=40 * 1024 * 1024
        ),
    )(*(pltpu.with_memory_space_constraint(x, pltpu.HBM) for x in operands))
    image, drop = pl.pallas_call(
        finish,
        out_shape=(
            jax.ShapeDtypeStruct((TT, WEEKS * PROBES, CELLS), F32),
            jax.ShapeDtypeStruct((TT, WEEKS, CELLS), F32),
        ),
        in_specs=[vmem] * 3,
        out_specs=(hbm, hbm),
        scratch_shapes=[
            pltpu.VMEM((TT, WEEKS * PROBES, CELLS), F32),
            pltpu.VMEM((TT, WEEKS, CELLS), F32),
            dma(TT + 1),
        ],
        compiler_params=pltpu.CompilerParams(vmem_limit_bytes=4 * 1024 * 1024),
    )(carried, spatial, probes.reshape(TT, WEEKS * PROBES, CELLS))
    return image.reshape(TT, WEEKS, PROBES, CELLS), drop


def solution(mesh):
    placed = (
        P(("snd", "cell"), None, None, None),
        P(("snd", "cell"), None, None),
        P(("snd", "cell")),
        P("snd", None),
        P("snd", None),
        P("snd", None, None),
        P("snd"),
    )
    return jax.shard_map(
        per_device,
        mesh=mesh,
        in_specs=placed,
        out_specs=(P(("snd", "cell"), None, None, None), P(("snd", "cell"), None, None)),
        check_vma=False,
    )
```

```python
import functools

import jax
import jax.numpy as jnp
from jax import lax
from jax.experimental import pallas as pl
from jax.experimental.pallas import tpu as pltpu
from jax.sharding import PartitionSpec as P

BF = jnp.bfloat16
F32 = jnp.float32
MESH = pl.DeviceIdType.MESH

TT = 8
SLOTS = 64
WEEKS = 4
PROBES = 32
CELLS = 128
SIDE = 2


def dot_nn(a, b):
    return lax.dot_general(a, b, (((1,), (0,)), ((), ())), preferred_element_type=F32)


def dot_nt(a, b):
    return lax.dot_general(a, b, (((1,), (1,)), ((), ())), preferred_element_type=F32)


def iota(shape, dim):
    return lax.broadcasted_iota(jnp.int32, shape, dim)


def low_half(rows):
    return iota((rows, 128), 1) < 64


def packed(values):
    low = low_half(16)
    rows = []
    for lanes in (slice(0, 128), slice(128, 256)):
        upper, lower = values[:16, lanes], values[16:, lanes]
        rows.append(jnp.where(low, upper, pltpu.roll(lower, 64, 1)))
        rows.append(jnp.where(low, pltpu.roll(upper, 64, 1), lower))
    return jnp.stack(rows).astype(BF)


def unpacked(block):
    low = low_half(16)
    wide = block.astype(F32)
    cols = []
    for even, odd in ((wide[0], wide[1]), (wide[2], wide[3])):
        upper = jnp.where(low, even, pltpu.roll(odd, 64, 1))
        lower = jnp.where(low, pltpu.roll(even, 64, 1), odd)
        cols.append(jnp.concatenate([upper, lower], axis=0))
    return jnp.concatenate(cols, axis=1)


def doubled(ranks):
    rows, cols = ranks.shape
    wide = ranks.reshape(rows // 8, 8, cols)
    return jnp.concatenate([wide, wide - 1.0], axis=1).reshape(2 * rows, cols).astype(BF)


def one_hot(*ranks):
    rows, cols = ranks[0].shape
    wide = [r.reshape(rows // 16, 16, cols) for r in ranks]
    one, zero = jnp.ones((), BF), jnp.zeros((), BF)
    rows_of = []
    for q in range(4):
        same = wide[0] == jnp.asarray(2 * q, BF)
        for r in wide[1:]:
            same = same | (r == jnp.asarray(2 * q, BF))
        rows_of.append(jnp.where(same, one, zero))
    return jnp.concatenate(rows_of, axis=1).reshape(4 * rows, cols)


def kernel(
    ns, nc, sound,
    probes_hbm, spatial_hbm, rho_hbm, tile_hbm, week_hbm, foot_hbm, sigma_hbm,
    carried_ref,
    probes_ref, spatial_ref, rho_ref, tile_ref, week_ref, foot_ref, sigma_ref, order_ref, early_ref, ranks_ref, hot_ref, field_ref, wide_ref,
    send_f, recv_f, send_k, recv_k, send_v, recv_v, send_p, recv_p,
    send_c, recv_c, send_y, recv_y, recv_w,
    load_sem, ss_f, rs_f, ss_k, rs_k, ss_v, rs_v, ss_p, rs_p, ss_c, rs_c, ss_y, rs_y, ss_w, rs_w,
):
    me = lax.axis_index("snd")
    mine = lax.axis_index("cell")
    core, row_y = mine % 2, mine // 2
    nj = ns * TT
    groups = ns // 4
    ny = nc // 2
    half = sound // 2
    mx, mz = me // 4, me % 4
    near = {1: [0], 2: [0, 1], 4: [0, 1, 3, 2]}[groups]
    far = near[::-1]
    far_z = [2, 1, 3, 0]

    loads = [
        pltpu.make_async_copy(src, dst, load_sem.at[i])
        for i, (src, dst) in enumerate(
            (
                (tile_hbm, tile_ref),
                (week_hbm, week_ref),
                (foot_hbm, foot_ref),
                (spatial_hbm, spatial_ref),
                (probes_hbm, probes_ref),
                (sigma_hbm, sigma_ref),
                (rho_hbm, rho_ref),
            )
        )
    ]
    for load in loads:
        load.start()

    barrier = pltpu.get_barrier_semaphore()

    def greet(snd, cell):
        pl.semaphore_signal(barrier, inc=1, device_id={"snd": snd, "cell": cell}, device_id_type=MESH)

    def group_x(dx):
        return (mx + dx) % groups

    def partner(dx, dz):
        return group_x(dx) * 4 + (mz + dz) % 4

    for dx in far:
        for dz in far_z:
            if (dx, dz) != (0, 0):
                greet(partner(dx, dz), mine)
    for dy in range(1, ny):
        greet(me, (row_y + dy) % ny * 2 + core)
    greet(me, row_y * 2 + 1 - core)

    def to_snd(refs, dest):
        src, dst, ss, rs = refs
        return pltpu.make_async_remote_copy(
            src_ref=src.at[dest], dst_ref=dst.at[me], send_sem=ss, recv_sem=rs,
            device_id={"snd": dest, "cell": mine}, device_id_type=MESH,
        )

    of_f = (send_f, recv_f, ss_f, rs_f)
    of_k = (send_k, recv_k, ss_k, rs_k)
    of_v = (send_v, recv_v, ss_v, rs_v)
    of_p = (send_p, recv_p, ss_p, rs_p)

    def send_group(refs, dx):
        for dz in far_z:
            if (dx, dz) != (0, 0):
                to_snd(refs, partner(dx, dz)).start()
        if dx == 0:
            refs[1][me] = refs[0][me]

    def of_others(buffer, sem):
        pltpu.make_async_copy(buffer.at[pl.ds(0, ns - 1)], buffer.at[pl.ds(0, ns - 1)], sem).wait()

    def arrived(refs):
        of_others(refs[1], refs[3])

    def sent(refs):
        of_others(refs[0], refs[2])

    def group_rows(dx, size):
        return pl.ds(pl.multiple_of(group_x(dx) * 4 * size, 4 * size), 4 * size)

    def group_of(dx):
        return pl.ds(pl.multiple_of(group_x(dx) * 4, 4), 4)

    loads[0].wait()
    loads[1].wait()
    tiles = tile_ref[...]
    weeks = week_ref[...]
    shift = nc.bit_length() - 1
    width = min(256, sound // 2)
    row_j = iota((nj, width), 0)
    upper = jnp.where(iota((width, width), 0) < iota((width, width), 1), 1.0, 0.0).astype(BF)
    counts = jnp.concatenate([upper, jnp.ones((width, width), BF)], axis=1)
    spread_e = jnp.where(iota((128, 512), 0) == iota((128, 512), 1) >> 2, 1.0, 0.0).astype(BF)
    pick_k = (iota((WEEKS, 512), 1) & 3) == iota((WEEKS, 512), 0)
    row_e = iota((nj, 512), 0).astype(F32)

    matched = ((tiles >> 3) & (nc - 1)) == mine
    local = jnp.where(matched, ((tiles >> (3 + shift)) << 3) | (tiles & 7), -1)
    carry = jnp.zeros((nj, width), F32)
    bits = jnp.zeros((nj, width), F32)
    for b in range(sound // width):
        if 2 * width * b == sound:
            early_ref[...] = carry[:, :128]
        lanes = slice(width * b, width * b + width)
        named = jnp.zeros((nj, width), F32)
        week_of = jnp.zeros((nj, width), jnp.int32)
        for k in range(4):
            same = local[k : k + 1, lanes] == row_j
            named = jnp.where(same, 1.0, named)
            week_of = jnp.where(same, weeks[k : k + 1, lanes], week_of)
        counted = dot_nn(named.astype(BF), counts)
        place = counted[:, :width] + carry
        order = jnp.where(named > 0.0, place, -1.0)
        carry = carry + counted[:, width:]
        bits = bits + (week_of << (place.astype(jnp.int32) * 2)).astype(F32)
        order_ref[:, lanes] = order
        for part in range(width // 128):
            a = width // 128 * b + part
            here = slice(128 * a, 128 * a + 128)
            spread_rank = dot_nn(order[:, 128 * part : 128 * part + 128].astype(BF), spread_e)
            spread_tile = dot_nn(local[:, here].astype(F32).astype(BF), spread_e)
            tile_e = jnp.sum(jnp.where(pick_k, spread_tile, 0.0), axis=0, keepdims=True)
            ranks_ref[a] = doubled(jnp.where(tile_e == row_e, spread_rank, -1.0))

    bits = jnp.sum(bits, axis=1, keepdims=True).astype(jnp.int32)
    lane = iota((TT, 128), 1)
    for d in range(ns):
        word = jnp.broadcast_to(bits[TT * d : TT * d + TT], (TT, 128))
        week = (word >> (((lane & 63) >> 3) * 2)) & 3
        row = jnp.sum(jnp.where((lane & 7) == iota((TT, 128), 0), week.astype(F32), 0.0), axis=0, keepdims=True)
        send_k[d] = row

    loads[2].wait()

    both = jnp.concatenate([foot_ref[: 2 * sound, :], foot_ref[2 * sound :, :]], axis=1)
    pairs = sound // 256

    def pick_feet(dx):
        for part in range(2):
            first = group_x(dx) * 4 + 2 * part
            rows = pl.ds(pl.multiple_of(first * 16, 32), 32)
            picks = [one_hot(ranks_ref[a, rows, :], ranks_ref[a + pairs, rows, :]) for a in range(pairs)]
            found = dot_nn(jnp.concatenate(picks, axis=1), both).reshape(2, 8, TT, 2 * CELLS)
            early = early_ref[pl.ds(pl.multiple_of(first * TT, 16), 16), :].reshape(2, TT, CELLS)
            kept = [jnp.where(early > float(r), found[:, r, :, :CELLS], found[:, r, :, CELLS:]) for r in range(8)]
            send_f[pl.ds(first, 2)] = jnp.stack(kept, axis=1).reshape(2, SLOTS, CELLS).astype(BF)

    for dx in far[: groups // 2]:
        pick_feet(dx)
    if groups == 1:
        pick_feet(0)
    pl.semaphore_wait(barrier, ns - 1 + ny - 1 + 1)
    for dx in far:
        send_group(of_k, dx)
    for dx in far[: groups // 2]:
        send_group(of_f, dx)
    for dx in far[groups // 2 :]:
        if groups > 1:
            pick_feet(dx)
        send_group(of_f, dx)

    for b in range(sound // 256):
        lanes = slice(256 * b, 256 * b + 256)
        hot_ref[:, lanes] = one_hot(doubled(order_ref[:, lanes]))

    for load in loads[3:]:
        load.wait()
    for t in range(TT):
        spread = dot_nt(probes_ref[t], spatial_ref[t])
        lanes = slice(CELLS * (t % SIDE), CELLS * (t % SIDE) + CELLS)
        running = spread[:PROBES]
        field_ref[t // SIDE, :PROBES, lanes] = running.astype(BF)
        for w in range(1, WEEKS):
            running = spread[PROBES * w : PROBES * w + PROBES] + rho_ref[t] * running
            field_ref[t // SIDE, PROBES * w : PROBES * w + PROBES, lanes] = running.astype(BF)

    lane_side = (iota((PROBES, 256), 1) & 7) // SIDE
    row_tile = (iota((256, CELLS), 0) & (SIDE - 1)).astype(F32).astype(BF)
    fields = field_ref[...].reshape(TT // SIDE * WEEKS * PROBES, SIDE * CELLS)
    codes = {}
    arrived(of_f)
    arrived(of_k)
    for dx in near:
        names = recv_k[group_of(dx)]
        low = low_half(1)
        code = jnp.concatenate([jnp.where(low, names[0], names[1]), jnp.where(low, names[2], names[3])], axis=1)
        codes[dx] = jnp.broadcast_to(code, (PROBES, 256))
        feet = recv_f[group_of(dx)].reshape(256, CELLS)
        sides = [jnp.where(row_tile == jnp.asarray(h, BF), feet, jnp.zeros((), BF)) for h in range(SIDE)]
        wide = jnp.concatenate(sides, axis=1)
        wide_ref[group_rows(dx, SLOTS), :] = wide
        full = dot_nt(fields, wide)
        full = full.reshape(TT // SIDE, WEEKS, PROBES, 256)
        value = jnp.zeros((PROBES, 256), F32)
        for w in range(WEEKS):
            here = full[0, w]
            for g in range(1, TT // SIDE):
                here = jnp.where(lane_side == g, full[g, w], here)
            value = jnp.where(codes[dx] == float(w), here, value)
        send_v[group_of(dx)] = packed(value)
    for dx in far:
        send_group(of_v, dx)

    sent(of_f)
    sent(of_k)

    seen = jnp.zeros((PROBES, sound), F32)
    arrived(of_v)
    for dx in near:
        seen = seen + dot_nn(unpacked(recv_v[group_of(dx)]).astype(BF), hot_ref[group_rows(dx, SLOTS), :])
    send_c[0] = seen[:, :half]
    send_c[1] = seen[:, half:]
    other_core = {"snd": me, "cell": row_y * 2 + 1 - core}
    swap = pltpu.make_async_remote_copy(
        src_ref=send_c.at[1 - core], dst_ref=recv_c, send_sem=ss_c, recv_sem=rs_c,
        device_id=other_core, device_id_type=MESH,
    )
    swap.start()
    swap.wait_recv()
    total = send_c[core] + recv_c[...]
    send_y[...] = total.astype(BF)

    def over_y(dy, slot):
        return pltpu.make_async_remote_copy(
            src_ref=send_y, dst_ref=recv_y.at[slot], send_sem=ss_y.at[dy], recv_sem=rs_y.at[slot],
            device_id={"snd": me, "cell": (row_y + dy) % ny * 2 + core}, device_id_type=MESH,
        )

    steps_y = {1: [], 2: [1], 4: [2, 1, 3]}[ny]
    for dy in steps_y:
        over_y(dy, row_y).start()
    sent(of_v)
    swap.wait_send()
    for dy in reversed(steps_y):
        over_y(dy, (row_y + dy) % ny).wait_recv()
    for dy in reversed(steps_y):
        total = total + recv_y[(row_y + dy) % ny].astype(F32)
    own = half // 128
    sigma = jnp.concatenate([sigma_ref[pl.ds(core * own + i, 1), :] for i in range(own)], axis=1)
    recv_w[core] = (total / (sigma * sigma)).astype(BF)
    share = pltpu.make_async_remote_copy(
        src_ref=recv_w.at[core], dst_ref=recv_w.at[core], send_sem=ss_w, recv_sem=rs_w,
        device_id=other_core, device_id_type=MESH,
    )
    share.start()
    share.wait_recv()

    weighted = jnp.concatenate([recv_w[0], recv_w[1]], axis=1)
    backs = dot_nt(weighted, hot_ref[...])
    for x in range(groups):
        send_p[4 * x : 4 * x + 4] = packed(backs[:, 256 * x : 256 * x + 256])
    for dx in far:
        send_group(of_p, dx)

    for dy in steps_y:
        over_y(dy, row_y).wait_send()

    at_side = [lane_side.astype(F32).astype(BF) == jnp.asarray(g, BF) for g in range(TT // SIDE)]
    arrived(of_p)
    spread = []
    for dx in near:
        value, code = unpacked(recv_p[group_of(dx)]).astype(BF), codes[dx].astype(BF)
        by_week = [jnp.where(code == jnp.asarray(w, BF), value, jnp.zeros((), BF)) for w in range(WEEKS)]
        spread.append([[jnp.where(at, part, jnp.zeros((), BF)) for part in by_week] for at in at_side])
    feet = jnp.concatenate([wide_ref[group_rows(dx, SLOTS), :] for dx in near], axis=0)
    for g in range(TT // SIDE):
        kept = jnp.concatenate([jnp.concatenate(parts[g], axis=0) for parts in spread], axis=1)
        adjoint = dot_nn(kept, feet)
        for h in range(SIDE):
            here = adjoint[:, CELLS * h : CELLS * h + CELLS]
            running = here[PROBES * (WEEKS - 1) :]
            carried = [running]
            for w in range(WEEKS - 2, -1, -1):
                running = here[PROBES * w : PROBES * w + PROBES] + rho_ref[SIDE * g + h] * running
                carried.append(running)
            carried_ref[SIDE * g + h] = jnp.concatenate(carried[::-1], axis=0).astype(BF)

    sent(of_p)
    share.wait_send()


def finish(carried_ref, spatial_ref, probes_ref, image_hbm, drop_hbm, image_ref, drop_ref, sems):
    stores = [pltpu.make_async_copy(image_ref.at[t], image_hbm.at[t], sems.at[t]) for t in range(TT)]
    for t in range(TT):
        image = dot_nn(carried_ref[t], spatial_ref[t])
        image_ref[t] = image
        stores[t].start()
        product = (probes_ref[t].astype(F32) * image).reshape(WEEKS, PROBES, CELLS)
        drop_ref[t] = jnp.sum(product, axis=1) * (1.0 / PROBES)
    last = pltpu.make_async_copy(drop_ref, drop_hbm, sems.at[TT])
    last.start()
    for store in stores:
        store.wait()
    last.wait()


def per_device(probes, spatial, rho, foot_tile, foot_week, footprint, sigma):
    ns, nc = lax.axis_size("snd"), lax.axis_size("cell")
    sound = foot_tile.shape[0]
    half = sound // 2
    hbm = pl.BlockSpec(memory_space=pltpu.HBM)
    vmem = pl.BlockSpec(memory_space=pltpu.VMEM)
    one = pltpu.SemaphoreType.DMA
    dma = lambda n: pltpu.SemaphoreType.DMA((n,))
    operands = (
        probes.reshape(TT, WEEKS * PROBES, CELLS),
        spatial,
        rho,
        foot_tile.T,
        foot_week.T,
        footprint.reshape(sound * 4, CELLS),
        sigma.reshape(sound // 128, 128),
    )
    carried = pl.pallas_call(
        functools.partial(kernel, ns, nc, sound),
        out_shape=jax.ShapeDtypeStruct((TT, WEEKS * PROBES, CELLS), BF),
        in_specs=[hbm] * 7,
        out_specs=vmem,
        scratch_shapes=[
            pltpu.VMEM((TT, WEEKS * PROBES, CELLS), BF),
            pltpu.VMEM((TT, CELLS, CELLS), BF),
            pltpu.SMEM((TT,), F32),
            pltpu.VMEM((4, sound), jnp.int32),
            pltpu.VMEM((4, sound), jnp.int32),
            pltpu.VMEM((sound * 4, CELLS), BF),
            pltpu.VMEM((sound // 128, 128), F32),
            pltpu.VMEM((ns * TT, sound), F32),
            pltpu.VMEM((ns * TT, 128), F32),
            pltpu.VMEM((sound // 128, ns * 16, 512), BF),
            pltpu.VMEM((ns * SLOTS, sound), BF),
            pltpu.VMEM((TT // SIDE, WEEKS * PROBES, SIDE * CELLS), BF),
            pltpu.VMEM((ns * SLOTS, SIDE * CELLS), BF),
            pltpu.VMEM((ns, SLOTS, CELLS), BF),
            pltpu.VMEM((ns, SLOTS, CELLS), BF),
            pltpu.VMEM((ns, 1, 128), F32),
            pltpu.VMEM((ns, 1, 128), F32),
            pltpu.VMEM((ns, 16, 128), BF),
            pltpu.VMEM((ns, 16, 128), BF),
            pltpu.VMEM((ns, 16, 128), BF),
            pltpu.VMEM((ns, 16, 128), BF),
            pltpu.VMEM((2, PROBES, half), F32),
            pltpu.VMEM((PROBES, half), F32),
            pltpu.VMEM((PROBES, half), BF),
            pltpu.VMEM((nc // 2, PROBES, half), BF),
            pltpu.VMEM((2, PROBES, half), BF),
            dma(7),
            one, one, one, one, one, one, one, one,
            one, one, dma(max(2, nc // 2)), dma(nc // 2), one, one,
        ],
        compiler_params=pltpu.CompilerParams(
            collective_id=0, has_side_effects=True, vmem_limit_bytes=40 * 1024 * 1024
        ),
    )(*(pltpu.with_memory_space_constraint(x, pltpu.HBM) for x in operands))
    image, drop = pl.pallas_call(
        finish,
        out_shape=(
            jax.ShapeDtypeStruct((TT, WEEKS * PROBES, CELLS), F32),
            jax.ShapeDtypeStruct((TT, WEEKS, CELLS), F32),
        ),
        in_specs=[vmem] * 3,
        out_specs=(hbm, hbm),
        scratch_shapes=[
            pltpu.VMEM((TT, WEEKS * PROBES, CELLS), F32),
            pltpu.VMEM((TT, WEEKS, CELLS), F32),
            dma(TT + 1),
        ],
        compiler_params=pltpu.CompilerParams(vmem_limit_bytes=4 * 1024 * 1024),
    )(carried, spatial, probes.reshape(TT, WEEKS * PROBES, CELLS))
    return image.reshape(TT, WEEKS, PROBES, CELLS), drop


def solution(mesh):
    placed = (
        P(("snd", "cell"), None, None, None),
        P(("snd", "cell"), None, None),
        P(("snd", "cell")),
        P("snd", None),
        P("snd", None),
        P("snd", None, None),
        P("snd"),
    )
    return jax.shard_map(
        per_device,
        mesh=mesh,
        in_specs=placed,
        out_specs=(P(("snd", "cell"), None, None, None), P(("snd", "cell"), None, None)),
        check_vma=False,
    )
```

```python
import functools

import jax
import jax.numpy as jnp
from jax import lax
from jax.experimental import pallas as pl
from jax.experimental.pallas import tpu as pltpu
from jax.sharding import PartitionSpec as P

BF = jnp.bfloat16
F32 = jnp.float32
MESH = pl.DeviceIdType.MESH

TT = 8
SLOTS = 64
WEEKS = 4
PROBES = 32
CELLS = 128
SIDE = 2


def dot_nn(a, b):
    return lax.dot_general(a, b, (((1,), (0,)), ((), ())), preferred_element_type=F32)


def dot_nt(a, b):
    return lax.dot_general(a, b, (((1,), (1,)), ((), ())), preferred_element_type=F32)


def iota(shape, dim):
    return lax.broadcasted_iota(jnp.int32, shape, dim)


def low_half(rows):
    return iota((rows, 128), 1) < 64


def packed(values):
    low = low_half(16)
    rows = []
    for lanes in (slice(0, 128), slice(128, 256)):
        upper, lower = values[:16, lanes], values[16:, lanes]
        rows.append(jnp.where(low, upper, pltpu.roll(lower, 64, 1)))
        rows.append(jnp.where(low, pltpu.roll(upper, 64, 1), lower))
    return jnp.stack(rows).astype(BF)


def unpacked(block):
    low = low_half(16)
    wide = block.astype(F32)
    cols = []
    for even, odd in ((wide[0], wide[1]), (wide[2], wide[3])):
        upper = jnp.where(low, even, pltpu.roll(odd, 64, 1))
        lower = jnp.where(low, pltpu.roll(even, 64, 1), odd)
        cols.append(jnp.concatenate([upper, lower], axis=0))
    return jnp.concatenate(cols, axis=1)


def doubled(ranks):
    rows, cols = ranks.shape
    wide = ranks.reshape(rows // 8, 8, cols)
    return jnp.concatenate([wide, wide - 1.0], axis=1).reshape(2 * rows, cols).astype(BF)


def one_hot(*ranks):
    rows, cols = ranks[0].shape
    wide = [r.reshape(rows // 16, 16, cols) for r in ranks]
    one, zero = jnp.ones((), BF), jnp.zeros((), BF)
    rows_of = []
    for q in range(4):
        same = wide[0] == jnp.asarray(2 * q, BF)
        for r in wide[1:]:
            same = same | (r == jnp.asarray(2 * q, BF))
        rows_of.append(jnp.where(same, one, zero))
    return jnp.concatenate(rows_of, axis=1).reshape(4 * rows, cols)


def kernel(
    ns, nc, sound,
    probes_hbm, spatial_hbm, rho_hbm, tile_hbm, week_hbm, foot_hbm, sigma_hbm,
    carried_ref,
    probes_ref, spatial_ref, rho_ref, tile_ref, week_ref, foot_ref, sigma_ref, order_ref, early_ref, ranks_ref, hot_ref, field_ref, wide_ref,
    send_f, recv_f, send_k, recv_k, send_v, recv_v, send_p, recv_p,
    send_c, recv_c, send_y, recv_y, recv_w,
    load_sem, ss_f, rs_f, ss_k, rs_k, ss_v, rs_v, ss_p, rs_p, ss_c, rs_c, ss_y, rs_y, ss_w, rs_w,
):
    me = lax.axis_index("snd")
    mine = lax.axis_index("cell")
    core, row_y = lax.rem(mine, 2), lax.div(mine, 2)
    nj = ns * TT
    groups = ns // 4
    ny = nc // 2
    half = sound // 2
    mx, mz = lax.div(me, 4), lax.rem(me, 4)
    near = {1: [0], 2: [0, 1], 4: [0, 1, 3, 2]}[groups]
    far = near[::-1]
    far_z = [2, 1, 3, 0]

    loads = [
        pltpu.make_async_copy(src, dst, load_sem.at[i])
        for i, (src, dst) in enumerate(
            (
                (tile_hbm, tile_ref),
                (week_hbm, week_ref),
                (foot_hbm, foot_ref),
                (spatial_hbm, spatial_ref),
                (probes_hbm, probes_ref),
                (sigma_hbm, sigma_ref),
                (rho_hbm, rho_ref),
            )
        )
    ]
    for load in loads:
        load.start()

    barrier = pltpu.get_barrier_semaphore()

    def greet(snd, cell):
        pl.semaphore_signal(barrier, inc=1, device_id={"snd": snd, "cell": cell}, device_id_type=MESH)

    def group_x(dx):
        return lax.rem(mx + dx, groups)

    def partner(dx, dz):
        return group_x(dx) * 4 + lax.rem(mz + dz, 4)

    for dx in far:
        for dz in far_z:
            if (dx, dz) != (0, 0):
                greet(partner(dx, dz), mine)
    for dy in range(1, ny):
        greet(me, lax.rem(row_y + dy, ny) * 2 + core)
    greet(me, row_y * 2 + 1 - core)

    def to_snd(refs, dest):
        src, dst, ss, rs = refs
        return pltpu.make_async_remote_copy(
            src_ref=src.at[dest], dst_ref=dst.at[me], send_sem=ss, recv_sem=rs,
            device_id={"snd": dest, "cell": mine}, device_id_type=MESH,
        )

    of_f = (send_f, recv_f, ss_f, rs_f)
    of_k = (send_k, recv_k, ss_k, rs_k)
    of_v = (send_v, recv_v, ss_v, rs_v)
    of_p = (send_p, recv_p, ss_p, rs_p)

    def send_group(refs, dx):
        for dz in far_z:
            if (dx, dz) != (0, 0):
                to_snd(refs, partner(dx, dz)).start()
        if dx == 0:
            refs[1][me] = refs[0][me]

    def of_others(buffer, sem):
        pltpu.make_async_copy(buffer.at[pl.ds(0, ns - 1)], buffer.at[pl.ds(0, ns - 1)], sem).wait()

    def arrived(refs):
        of_others(refs[1], refs[3])

    def sent(refs):
        of_others(refs[0], refs[2])

    def group_rows(dx, size):
        return pl.ds(pl.multiple_of(group_x(dx) * 4 * size, 4 * size), 4 * size)

    def group_of(dx):
        return pl.ds(pl.multiple_of(group_x(dx) * 4, 4), 4)

    loads[0].wait()
    loads[1].wait()
    tiles = tile_ref[...]
    weeks = week_ref[...]
    shift = nc.bit_length() - 1
    width = min(256, sound // 2)
    row_j = iota((nj, width), 0)
    upper = jnp.where(iota((width, width), 0) < iota((width, width), 1), 1.0, 0.0).astype(BF)
    counts = jnp.concatenate([upper, jnp.ones((width, width), BF)], axis=1)
    spread_e = jnp.where(iota((128, 512), 0) == iota((128, 512), 1) >> 2, 1.0, 0.0).astype(BF)
    pick_k = (iota((WEEKS, 512), 1) & 3) == iota((WEEKS, 512), 0)
    row_e = iota((nj, 512), 0).astype(F32)

    matched = ((tiles >> 3) & (nc - 1)) == mine
    local = jnp.where(matched, ((tiles >> (3 + shift)) << 3) | (tiles & 7), -1)
    carry = jnp.zeros((nj, width), F32)
    bits = jnp.zeros((nj, width), F32)
    for b in range(sound // width):
        if 2 * width * b == sound:
            early_ref[...] = carry[:, :128]
        lanes = slice(width * b, width * b + width)
        named = jnp.zeros((nj, width), F32)
        week_of = jnp.zeros((nj, width), jnp.int32)
        for k in range(4):
            same = local[k : k + 1, lanes] == row_j
            named = jnp.where(same, 1.0, named)
            week_of = jnp.where(same, weeks[k : k + 1, lanes], week_of)
        counted = dot_nn(named.astype(BF), counts)
        place = counted[:, :width] + carry
        order = jnp.where(named > 0.0, place, -1.0)
        carry = carry + counted[:, width:]
        bits = bits + (week_of << (place.astype(jnp.int32) * 2)).astype(F32)
        order_ref[:, lanes] = order
        for part in range(width // 128):
            a = width // 128 * b + part
            here = slice(128 * a, 128 * a + 128)
            spread_rank = dot_nn(order[:, 128 * part : 128 * part + 128].astype(BF), spread_e)
            spread_tile = dot_nn(local[:, here].astype(F32).astype(BF), spread_e)
            tile_e = jnp.sum(jnp.where(pick_k, spread_tile, 0.0), axis=0, keepdims=True)
            ranks_ref[a] = doubled(jnp.where(tile_e == row_e, spread_rank, -1.0))

    bits = jnp.sum(bits, axis=1, keepdims=True).astype(jnp.int32)
    lane = iota((TT, 128), 1)
    for d in range(ns):
        word = jnp.broadcast_to(bits[TT * d : TT * d + TT], (TT, 128))
        week = (word >> (((lane & 63) >> 3) * 2)) & 3
        row = jnp.sum(jnp.where((lane & 7) == iota((TT, 128), 0), week.astype(F32), 0.0), axis=0, keepdims=True)
        send_k[d] = row

    loads[2].wait()

    both = jnp.concatenate([foot_ref[: 2 * sound, :], foot_ref[2 * sound :, :]], axis=1)
    pairs = sound // 256

    def pick_feet(dx):
        for part in range(2):
            first = group_x(dx) * 4 + 2 * part
            rows = pl.ds(pl.multiple_of(first * 16, 32), 32)
            picks = [one_hot(ranks_ref[a, rows, :], ranks_ref[a + pairs, rows, :]) for a in range(pairs)]
            found = dot_nn(jnp.concatenate(picks, axis=1), both).reshape(2, 8, TT, 2 * CELLS)
            early = early_ref[pl.ds(pl.multiple_of(first * TT, 16), 16), :].reshape(2, TT, CELLS)
            kept = [jnp.where(early > float(r), found[:, r, :, :CELLS], found[:, r, :, CELLS:]) for r in range(8)]
            send_f[pl.ds(first, 2)] = jnp.stack(kept, axis=1).reshape(2, SLOTS, CELLS).astype(BF)

    for dx in far[: groups // 2]:
        pick_feet(dx)
    if groups == 1:
        pick_feet(0)
    pl.semaphore_wait(barrier, ns - 1 + ny - 1 + 1)
    for dx in far:
        send_group(of_k, dx)
    for dx in far[: groups // 2]:
        send_group(of_f, dx)
    for dx in far[groups // 2 :]:
        if groups > 1:
            pick_feet(dx)
        send_group(of_f, dx)

    for b in range(sound // 256):
        lanes = slice(256 * b, 256 * b + 256)
        hot_ref[:, lanes] = one_hot(doubled(order_ref[:, lanes]))

    for load in loads[3:]:
        load.wait()
    for t in range(TT):
        spread = dot_nt(probes_ref[t], spatial_ref[t])
        lanes = slice(CELLS * (t % SIDE), CELLS * (t % SIDE) + CELLS)
        running = spread[:PROBES]
        field_ref[t // SIDE, :PROBES, lanes] = running.astype(BF)
        for w in range(1, WEEKS):
            running = spread[PROBES * w : PROBES * w + PROBES] + rho_ref[t] * running
            field_ref[t // SIDE, PROBES * w : PROBES * w + PROBES, lanes] = running.astype(BF)

    lane_side = (iota((PROBES, 256), 1) & 7) // SIDE
    row_tile = (iota((256, CELLS), 0) & (SIDE - 1)).astype(F32).astype(BF)
    fields = field_ref[...].reshape(TT // SIDE * WEEKS * PROBES, SIDE * CELLS)
    codes = {}
    arrived(of_f)
    arrived(of_k)
    for dx in near:
        names = recv_k[group_of(dx)]
        low = low_half(1)
        code = jnp.concatenate([jnp.where(low, names[0], names[1]), jnp.where(low, names[2], names[3])], axis=1)
        codes[dx] = jnp.broadcast_to(code, (PROBES, 256))
        feet = recv_f[group_of(dx)].reshape(256, CELLS)
        sides = [jnp.where(row_tile == jnp.asarray(h, BF), feet, jnp.zeros((), BF)) for h in range(SIDE)]
        wide = jnp.concatenate(sides, axis=1)
        wide_ref[group_rows(dx, SLOTS), :] = wide
        full = dot_nt(fields, wide)
        full = full.reshape(TT // SIDE, WEEKS, PROBES, 256)
        value = jnp.zeros((PROBES, 256), F32)
        for w in range(WEEKS):
            here = full[0, w]
            for g in range(1, TT // SIDE):
                here = jnp.where(lane_side == g, full[g, w], here)
            value = jnp.where(codes[dx] == float(w), here, value)
        send_v[group_of(dx)] = packed(value)
    for dx in far:
        send_group(of_v, dx)

    sent(of_f)
    sent(of_k)

    seen = jnp.zeros((PROBES, sound), F32)
    arrived(of_v)
    for dx in near:
        seen = seen + dot_nn(unpacked(recv_v[group_of(dx)]).astype(BF), hot_ref[group_rows(dx, SLOTS), :])
    send_c[0] = seen[:, :half]
    send_c[1] = seen[:, half:]
    other_core = {"snd": me, "cell": row_y * 2 + 1 - core}
    swap = pltpu.make_async_remote_copy(
        src_ref=send_c.at[1 - core], dst_ref=recv_c, send_sem=ss_c, recv_sem=rs_c,
        device_id=other_core, device_id_type=MESH,
    )
    swap.start()
    swap.wait_recv()
    total = send_c[core] + recv_c[...]
    send_y[...] = total.astype(BF)

    def over_y(dy, slot):
        return pltpu.make_async_remote_copy(
            src_ref=send_y, dst_ref=recv_y.at[slot], send_sem=ss_y.at[dy], recv_sem=rs_y.at[slot],
            device_id={"snd": me, "cell": lax.rem(row_y + dy, ny) * 2 + core}, device_id_type=MESH,
        )

    steps_y = {1: [], 2: [1], 4: [2, 1, 3]}[ny]
    for dy in steps_y:
        over_y(dy, row_y).start()
    sent(of_v)
    swap.wait_send()
    for dy in reversed(steps_y):
        over_y(dy, lax.rem(row_y + dy, ny)).wait_recv()
    for dy in reversed(steps_y):
        total = total + recv_y[lax.rem(row_y + dy, ny)].astype(F32)
    own = half // 128
    sigma = jnp.concatenate([sigma_ref[pl.ds(core * own + i, 1), :] for i in range(own)], axis=1)
    recv_w[core] = (total / (sigma * sigma)).astype(BF)
    share = pltpu.make_async_remote_copy(
        src_ref=recv_w.at[core], dst_ref=recv_w.at[core], send_sem=ss_w, recv_sem=rs_w,
        device_id=other_core, device_id_type=MESH,
    )
    share.start()
    share.wait_recv()

    weighted = jnp.concatenate([recv_w[0], recv_w[1]], axis=1)
    backs = dot_nt(weighted, hot_ref[...])
    for x in range(groups):
        send_p[4 * x : 4 * x + 4] = packed(backs[:, 256 * x : 256 * x + 256])
    for dx in far:
        send_group(of_p, dx)

    for dy in steps_y:
        over_y(dy, row_y).wait_send()

    at_side = [lane_side.astype(F32).astype(BF) == jnp.asarray(g, BF) for g in range(TT // SIDE)]
    arrived(of_p)
    spread = []
    for dx in near:
        value, code = unpacked(recv_p[group_of(dx)]).astype(BF), codes[dx].astype(BF)
        by_week = [jnp.where(code == jnp.asarray(w, BF), value, jnp.zeros((), BF)) for w in range(WEEKS)]
        spread.append([[jnp.where(at, part, jnp.zeros((), BF)) for part in by_week] for at in at_side])
    feet = jnp.concatenate([wide_ref[group_rows(dx, SLOTS), :] for dx in near], axis=0)
    for g in range(TT // SIDE):
        kept = jnp.concatenate([jnp.concatenate(parts[g], axis=0) for parts in spread], axis=1)
        adjoint = dot_nn(kept, feet)
        for h in range(SIDE):
            here = adjoint[:, CELLS * h : CELLS * h + CELLS]
            running = here[PROBES * (WEEKS - 1) :]
            carried = [running]
            for w in range(WEEKS - 2, -1, -1):
                running = here[PROBES * w : PROBES * w + PROBES] + rho_ref[SIDE * g + h] * running
                carried.append(running)
            carried_ref[SIDE * g + h] = jnp.concatenate(carried[::-1], axis=0).astype(BF)

    sent(of_p)
    share.wait_send()


def finish(carried_ref, spatial_ref, probes_ref, image_hbm, drop_hbm, image_ref, drop_ref, sems):
    stores = [
        pltpu.make_async_copy(image_ref.at[pl.ds(t, 2)], image_hbm.at[pl.ds(t, 2)], sems.at[t]) for t in range(0, TT, 2)
    ]
    stores.append(pltpu.make_async_copy(drop_ref, drop_hbm, sems.at[TT]))
    images = []
    for t in range(TT):
        images.append(dot_nn(carried_ref[t], spatial_ref[t]))
        image_ref[t] = images[t]
        if t % 2:
            stores[t // 2].start()
    for t in range(TT):
        product = (probes_ref[t].astype(F32) * images[t]).reshape(WEEKS, PROBES, CELLS)
        drop_ref[t] = jnp.sum(product, axis=1) * (1.0 / PROBES)
    stores[-1].start()
    for store in stores:
        store.wait()


def per_device(probes, spatial, rho, foot_tile, foot_week, footprint, sigma):
    ns, nc = lax.axis_size("snd"), lax.axis_size("cell")
    sound = foot_tile.shape[0]
    half = sound // 2
    hbm = pl.BlockSpec(memory_space=pltpu.HBM)
    vmem = pl.BlockSpec(memory_space=pltpu.VMEM)
    one = pltpu.SemaphoreType.DMA
    dma = lambda n: pltpu.SemaphoreType.DMA((n,))
    operands = (
        probes.reshape(TT, WEEKS * PROBES, CELLS),
        spatial,
        rho,
        foot_tile.T,
        foot_week.T,
        footprint.reshape(sound * 4, CELLS),
        sigma.reshape(sound // 128, 128),
    )
    carried = pl.pallas_call(
        functools.partial(kernel, ns, nc, sound),
        out_shape=jax.ShapeDtypeStruct((TT, WEEKS * PROBES, CELLS), BF),
        in_specs=[hbm] * 7,
        out_specs=vmem,
        scratch_shapes=[
            pltpu.VMEM((TT, WEEKS * PROBES, CELLS), BF),
            pltpu.VMEM((TT, CELLS, CELLS), BF),
            pltpu.SMEM((TT,), F32),
            pltpu.VMEM((4, sound), jnp.int32),
            pltpu.VMEM((4, sound), jnp.int32),
            pltpu.VMEM((sound * 4, CELLS), BF),
            pltpu.VMEM((sound // 128, 128), F32),
            pltpu.VMEM((ns * TT, sound), F32),
            pltpu.VMEM((ns * TT, 128), F32),
            pltpu.VMEM((sound // 128, ns * 16, 512), BF),
            pltpu.VMEM((ns * SLOTS, sound), BF),
            pltpu.VMEM((TT // SIDE, WEEKS * PROBES, SIDE * CELLS), BF),
            pltpu.VMEM((ns * SLOTS, SIDE * CELLS), BF),
            pltpu.VMEM((ns, SLOTS, CELLS), BF),
            pltpu.VMEM((ns, SLOTS, CELLS), BF),
            pltpu.VMEM((ns, 1, 128), F32),
            pltpu.VMEM((ns, 1, 128), F32),
            pltpu.VMEM((ns, 16, 128), BF),
            pltpu.VMEM((ns, 16, 128), BF),
            pltpu.VMEM((ns, 16, 128), BF),
            pltpu.VMEM((ns, 16, 128), BF),
            pltpu.VMEM((2, PROBES, half), F32),
            pltpu.VMEM((PROBES, half), F32),
            pltpu.VMEM((PROBES, half), BF),
            pltpu.VMEM((nc // 2, PROBES, half), BF),
            pltpu.VMEM((2, PROBES, half), BF),
            dma(7),
            one, one, one, one, one, one, one, one,
            one, one, dma(max(2, nc // 2)), dma(nc // 2), one, one,
        ],
        compiler_params=pltpu.CompilerParams(
            collective_id=0, has_side_effects=True, vmem_limit_bytes=40 * 1024 * 1024
        ),
    )(*(pltpu.with_memory_space_constraint(x, pltpu.HBM) for x in operands))
    image, drop = pl.pallas_call(
        finish,
        out_shape=(
            jax.ShapeDtypeStruct((TT, WEEKS * PROBES, CELLS), F32),
            jax.ShapeDtypeStruct((TT, WEEKS, CELLS), F32),
        ),
        in_specs=[vmem] * 3,
        out_specs=(hbm, hbm),
        scratch_shapes=[
            pltpu.VMEM((TT, WEEKS * PROBES, CELLS), F32),
            pltpu.VMEM((TT, WEEKS, CELLS), F32),
            dma(TT + 1),
        ],
        compiler_params=pltpu.CompilerParams(vmem_limit_bytes=4 * 1024 * 1024),
    )(carried, spatial, probes.reshape(TT, WEEKS * PROBES, CELLS))
    return image.reshape(TT, WEEKS, PROBES, CELLS), drop


def solution(mesh):
    placed = (
        P(("snd", "cell"), None, None, None),
        P(("snd", "cell"), None, None),
        P(("snd", "cell")),
        P("snd", None),
        P("snd", None),
        P("snd", None, None),
        P("snd"),
    )
    return jax.shard_map(
        per_device,
        mesh=mesh,
        in_specs=placed,
        out_specs=(P(("snd", "cell"), None, None, None), P(("snd", "cell"), None, None)),
        check_vma=False,
    )
```

```python
import functools

import jax
import jax.numpy as jnp
from jax import lax
from jax.experimental import pallas as pl
from jax.experimental.pallas import tpu as pltpu
from jax.sharding import PartitionSpec as P

BF = jnp.bfloat16
F32 = jnp.float32
MESH = pl.DeviceIdType.MESH

TT = 8
SLOTS = 64
WEEKS = 4
PROBES = 32
CELLS = 128
SIDE = 2


def dot_nn(a, b):
    return lax.dot_general(a, b, (((1,), (0,)), ((), ())), preferred_element_type=F32)


def dot_nt(a, b):
    return lax.dot_general(a, b, (((1,), (1,)), ((), ())), preferred_element_type=F32)


def iota(shape, dim):
    return lax.broadcasted_iota(jnp.int32, shape, dim)


def low_half(rows):
    return iota((rows, 128), 1) < 64


def packed(values):
    low = low_half(16)
    rows = []
    for lanes in (slice(0, 128), slice(128, 256)):
        upper, lower = values[:16, lanes], values[16:, lanes]
        rows.append(jnp.where(low, upper, pltpu.roll(lower, 64, 1)))
        rows.append(jnp.where(low, pltpu.roll(upper, 64, 1), lower))
    return jnp.stack(rows).astype(BF)


def unpacked(block):
    low = low_half(16)
    wide = block.astype(F32)
    cols = []
    for even, odd in ((wide[0], wide[1]), (wide[2], wide[3])):
        upper = jnp.where(low, even, pltpu.roll(odd, 64, 1))
        lower = jnp.where(low, pltpu.roll(even, 64, 1), odd)
        cols.append(jnp.concatenate([upper, lower], axis=0))
    return jnp.concatenate(cols, axis=1)


def doubled(ranks):
    rows, cols = ranks.shape
    wide = ranks.reshape(rows // 8, 8, cols)
    return jnp.concatenate([wide, wide - 1.0], axis=1).reshape(2 * rows, cols).astype(BF)


def one_hot(*ranks):
    rows, cols = ranks[0].shape
    wide = [r.reshape(rows // 16, 16, cols) for r in ranks]
    one, zero = jnp.ones((), BF), jnp.zeros((), BF)
    rows_of = []
    for q in range(4):
        same = wide[0] == jnp.asarray(2 * q, BF)
        for r in wide[1:]:
            same = same | (r == jnp.asarray(2 * q, BF))
        rows_of.append(jnp.where(same, one, zero))
    return jnp.concatenate(rows_of, axis=1).reshape(4 * rows, cols)


def kernel(
    ns, nc, sound,
    probes_hbm, spatial_hbm, rho_hbm, tile_hbm, week_hbm, foot_hbm, sigma_hbm,
    carried_ref,
    probes_ref, spatial_ref, rho_ref, tile_ref, week_ref, foot_ref, sigma_ref, order_ref, early_ref, ranks_ref, hot_ref, turned_ref, field_ref, wide_ref,
    send_f, recv_f, send_k, recv_k, send_v, recv_v, send_p, recv_p,
    send_c, recv_c, send_y, recv_y, recv_w,
    load_sem, ss_f, rs_f, ss_k, rs_k, ss_v, rs_v, ss_p, rs_p, ss_c, rs_c, ss_y, rs_y, ss_w, rs_w,
):
    me = lax.axis_index("snd")
    mine = lax.axis_index("cell")
    core, row_y = lax.rem(mine, 2), lax.div(mine, 2)
    nj = ns * TT
    groups = ns // 4
    ny = nc // 2
    half = sound // 2
    mx, mz = lax.div(me, 4), lax.rem(me, 4)
    near = {1: [0], 2: [0, 1], 4: [0, 1, 3, 2]}[groups]
    far = near[::-1]
    far_z = [2, 1, 3, 0]

    loads = [
        pltpu.make_async_copy(src, dst, load_sem.at[i])
        for i, (src, dst) in enumerate(
            (
                (tile_hbm, tile_ref),
                (week_hbm, week_ref),
                (foot_hbm, foot_ref),
                (spatial_hbm, spatial_ref),
                (probes_hbm, probes_ref),
                (sigma_hbm, sigma_ref),
                (rho_hbm, rho_ref),
            )
        )
    ]
    for load in loads:
        load.start()

    barrier = pltpu.get_barrier_semaphore()

    def greet(snd, cell):
        pl.semaphore_signal(barrier, inc=1, device_id={"snd": snd, "cell": cell}, device_id_type=MESH)

    def group_x(dx):
        return lax.rem(mx + dx, groups)

    def partner(dx, dz):
        return group_x(dx) * 4 + lax.rem(mz + dz, 4)

    for dx in far:
        for dz in far_z:
            if (dx, dz) != (0, 0):
                greet(partner(dx, dz), mine)
    for dy in range(1, ny):
        greet(me, lax.rem(row_y + dy, ny) * 2 + core)
    greet(me, row_y * 2 + 1 - core)

    def to_snd(refs, dest):
        src, dst, ss, rs = refs
        return pltpu.make_async_remote_copy(
            src_ref=src.at[dest], dst_ref=dst.at[me], send_sem=ss, recv_sem=rs,
            device_id={"snd": dest, "cell": mine}, device_id_type=MESH,
        )

    of_f = (send_f, recv_f, ss_f, rs_f)
    of_k = (send_k, recv_k, ss_k, rs_k)
    of_v = (send_v, recv_v, ss_v, rs_v)
    of_p = (send_p, recv_p, ss_p, rs_p)

    def send_group(refs, dx):
        for dz in far_z:
            if (dx, dz) != (0, 0):
                to_snd(refs, partner(dx, dz)).start()
        if dx == 0:
            refs[1][me] = refs[0][me]

    def of_others(buffer, sem):
        pltpu.make_async_copy(buffer.at[pl.ds(0, ns - 1)], buffer.at[pl.ds(0, ns - 1)], sem).wait()

    def arrived(refs):
        of_others(refs[1], refs[3])

    def sent(refs):
        of_others(refs[0], refs[2])

    def group_rows(dx, size):
        return pl.ds(pl.multiple_of(group_x(dx) * 4 * size, 4 * size), 4 * size)

    def group_of(dx):
        return pl.ds(pl.multiple_of(group_x(dx) * 4, 4), 4)

    loads[0].wait()
    loads[1].wait()
    tiles = tile_ref[...]
    weeks = week_ref[...]
    shift = nc.bit_length() - 1
    width = min(256, sound // 2)
    row_j = iota((nj, width), 0)
    upper = jnp.where(iota((width, width), 0) < iota((width, width), 1), 1.0, 0.0).astype(BF)
    counts = jnp.concatenate([upper, jnp.ones((width, width), BF)], axis=1)
    spread_e = jnp.where(iota((128, 512), 0) == iota((128, 512), 1) >> 2, 1.0, 0.0).astype(BF)
    pick_k = (iota((WEEKS, 512), 1) & 3) == iota((WEEKS, 512), 0)
    row_e = iota((nj, 512), 0).astype(F32)

    matched = ((tiles >> 3) & (nc - 1)) == mine
    local = jnp.where(matched, ((tiles >> (3 + shift)) << 3) | (tiles & 7), -1)
    carry = jnp.zeros((nj, width), F32)
    bits = jnp.zeros((nj, width), F32)
    for b in range(sound // width):
        if 2 * width * b == sound:
            early_ref[...] = carry[:, :128]
        lanes = slice(width * b, width * b + width)
        named = jnp.zeros((nj, width), F32)
        week_of = jnp.zeros((nj, width), jnp.int32)
        for k in range(4):
            same = local[k : k + 1, lanes] == row_j
            named = jnp.where(same, 1.0, named)
            week_of = jnp.where(same, weeks[k : k + 1, lanes], week_of)
        counted = dot_nn(named.astype(BF), counts)
        place = counted[:, :width] + carry
        order = jnp.where(named > 0.0, place, -1.0)
        carry = carry + counted[:, width:]
        bits = bits + (week_of << (place.astype(jnp.int32) * 2)).astype(F32)
        order_ref[:, lanes] = order
        for part in range(width // 128):
            a = width // 128 * b + part
            here = slice(128 * a, 128 * a + 128)
            spread_rank = dot_nn(order[:, 128 * part : 128 * part + 128].astype(BF), spread_e)
            spread_tile = dot_nn(local[:, here].astype(F32).astype(BF), spread_e)
            tile_e = jnp.sum(jnp.where(pick_k, spread_tile, 0.0), axis=0, keepdims=True)
            ranks_ref[a] = doubled(jnp.where(tile_e == row_e, spread_rank, -1.0))

    bits = jnp.sum(bits, axis=1, keepdims=True).astype(jnp.int32)
    lane = iota((TT, 128), 1)
    for d in range(ns):
        word = jnp.broadcast_to(bits[TT * d : TT * d + TT], (TT, 128))
        week = (word >> (((lane & 63) >> 3) * 2)) & 3
        row = jnp.sum(jnp.where((lane & 7) == iota((TT, 128), 0), week.astype(F32), 0.0), axis=0, keepdims=True)
        send_k[d] = row

    loads[2].wait()

    both = jnp.concatenate([foot_ref[: 2 * sound, :], foot_ref[2 * sound :, :]], axis=1)
    pairs = sound // 256

    def pick_feet(dx):
        for part in range(2):
            first = group_x(dx) * 4 + 2 * part
            rows = pl.ds(pl.multiple_of(first * 16, 32), 32)
            picks = [one_hot(ranks_ref[a, rows, :], ranks_ref[a + pairs, rows, :]) for a in range(pairs)]
            found = dot_nn(jnp.concatenate(picks, axis=1), both).reshape(2, 8, TT, 2 * CELLS)
            early = early_ref[pl.ds(pl.multiple_of(first * TT, 16), 16), :].reshape(2, TT, CELLS)
            kept = [jnp.where(early > float(r), found[:, r, :, :CELLS], found[:, r, :, CELLS:]) for r in range(8)]
            send_f[pl.ds(first, 2)] = jnp.stack(kept, axis=1).reshape(2, SLOTS, CELLS).astype(BF)

    for dx in far[: groups // 2]:
        pick_feet(dx)
    if groups == 1:
        pick_feet(0)
    pl.semaphore_wait(barrier, ns - 1 + ny - 1 + 1)
    for dx in far:
        send_group(of_k, dx)
    for dx in far[: groups // 2]:
        send_group(of_f, dx)
    for dx in far[groups // 2 :]:
        if groups > 1:
            pick_feet(dx)
        send_group(of_f, dx)

    for b in range(sound // 256):
        lanes = slice(256 * b, 256 * b + 256)
        hot_ref[:, lanes] = one_hot(doubled(order_ref[:, lanes]))
        turned_ref[lanes, :] = hot_ref[:, lanes].T

    for load in loads[3:]:
        load.wait()
    for t in range(TT):
        spread = dot_nt(probes_ref[t], spatial_ref[t])
        lanes = slice(CELLS * (t % SIDE), CELLS * (t % SIDE) + CELLS)
        running = spread[:PROBES]
        field_ref[t // SIDE, :PROBES, lanes] = running.astype(BF)
        for w in range(1, WEEKS):
            running = spread[PROBES * w : PROBES * w + PROBES] + rho_ref[t] * running
            field_ref[t // SIDE, PROBES * w : PROBES * w + PROBES, lanes] = running.astype(BF)

    lane_side = (iota((PROBES, 256), 1) & 7) // SIDE
    row_tile = (iota((256, CELLS), 0) & (SIDE - 1)).astype(F32).astype(BF)
    fields = field_ref[...].reshape(TT // SIDE * WEEKS * PROBES, SIDE * CELLS)
    codes = {}
    arrived(of_f)
    arrived(of_k)
    for dx in near:
        names = recv_k[group_of(dx)]
        low = low_half(1)
        code = jnp.concatenate([jnp.where(low, names[0], names[1]), jnp.where(low, names[2], names[3])], axis=1)
        codes[dx] = jnp.broadcast_to(code, (PROBES, 256))
        feet = recv_f[group_of(dx)].reshape(256, CELLS)
        sides = [jnp.where(row_tile == jnp.asarray(h, BF), feet, jnp.zeros((), BF)) for h in range(SIDE)]
        wide = jnp.concatenate(sides, axis=1)
        wide_ref[group_rows(dx, SLOTS), :] = wide
        full = dot_nt(fields, wide)
        full = full.reshape(TT // SIDE, WEEKS, PROBES, 256)
        value = jnp.zeros((PROBES, 256), F32)
        for w in range(WEEKS):
            here = full[0, w]
            for g in range(1, TT // SIDE):
                here = jnp.where(lane_side == g, full[g, w], here)
            value = jnp.where(codes[dx] == float(w), here, value)
        send_v[group_of(dx)] = packed(value)
    for dx in far:
        send_group(of_v, dx)

    sent(of_f)
    sent(of_k)

    seen = jnp.zeros((PROBES, sound), F32)
    arrived(of_v)
    for dx in near:
        seen = seen + dot_nn(unpacked(recv_v[group_of(dx)]).astype(BF), hot_ref[group_rows(dx, SLOTS), :])
    send_c[0] = seen[:, :half]
    send_c[1] = seen[:, half:]
    other_core = {"snd": me, "cell": row_y * 2 + 1 - core}
    swap = pltpu.make_async_remote_copy(
        src_ref=send_c.at[1 - core], dst_ref=recv_c, send_sem=ss_c, recv_sem=rs_c,
        device_id=other_core, device_id_type=MESH,
    )
    swap.start()
    swap.wait_recv()
    total = send_c[core] + recv_c[...]
    send_y[...] = total.astype(BF)

    def over_y(dy, slot):
        return pltpu.make_async_remote_copy(
            src_ref=send_y, dst_ref=recv_y.at[slot], send_sem=ss_y.at[dy], recv_sem=rs_y.at[slot],
            device_id={"snd": me, "cell": lax.rem(row_y + dy, ny) * 2 + core}, device_id_type=MESH,
        )

    steps_y = {1: [], 2: [1], 4: [2, 1, 3]}[ny]
    for dy in steps_y:
        over_y(dy, row_y).start()
    sent(of_v)
    swap.wait_send()
    for dy in reversed(steps_y):
        over_y(dy, lax.rem(row_y + dy, ny)).wait_recv()
    for dy in reversed(steps_y):
        total = total + recv_y[lax.rem(row_y + dy, ny)].astype(F32)
    own = half // 128
    sigma = jnp.concatenate([sigma_ref[pl.ds(core * own + i, 1), :] for i in range(own)], axis=1)
    recv_w[core] = (total / (sigma * sigma)).astype(BF)
    share = pltpu.make_async_remote_copy(
        src_ref=recv_w.at[core], dst_ref=recv_w.at[core], send_sem=ss_w, recv_sem=rs_w,
        device_id=other_core, device_id_type=MESH,
    )
    share.start()
    share.wait_recv()

    weighted = jnp.concatenate([recv_w[0], recv_w[1]], axis=1)
    backs = dot_nn(weighted, turned_ref[...])
    for x in range(groups):
        send_p[4 * x : 4 * x + 4] = packed(backs[:, 256 * x : 256 * x + 256])
    for dx in far:
        send_group(of_p, dx)

    for dy in steps_y:
        over_y(dy, row_y).wait_send()

    at_side = [lane_side.astype(F32).astype(BF) == jnp.asarray(g, BF) for g in range(TT // SIDE)]
    arrived(of_p)
    spread = []
    for dx in near:
        value, code = unpacked(recv_p[group_of(dx)]).astype(BF), codes[dx].astype(BF)
        by_week = [jnp.where(code == jnp.asarray(w, BF), value, jnp.zeros((), BF)) for w in range(WEEKS)]
        spread.append([[jnp.where(at, part, jnp.zeros((), BF)) for part in by_week] for at in at_side])
    feet = jnp.concatenate([wide_ref[group_rows(dx, SLOTS), :] for dx in near], axis=0)
    for g in range(TT // SIDE):
        kept = jnp.concatenate([jnp.concatenate(parts[g], axis=0) for parts in spread], axis=1)
        adjoint = dot_nn(kept, feet)
        for h in range(SIDE):
            here = adjoint[:, CELLS * h : CELLS * h + CELLS]
            running = here[PROBES * (WEEKS - 1) :]
            carried = [running]
            for w in range(WEEKS - 2, -1, -1):
                running = here[PROBES * w : PROBES * w + PROBES] + rho_ref[SIDE * g + h] * running
                carried.append(running)
            carried_ref[SIDE * g + h] = jnp.concatenate(carried[::-1], axis=0).astype(BF)

    sent(of_p)
    share.wait_send()


def finish(carried_ref, spatial_ref, probes_ref, image_hbm, drop_hbm, image_ref, drop_ref, sems):
    stores = [
        pltpu.make_async_copy(image_ref.at[pl.ds(t, 2)], image_hbm.at[pl.ds(t, 2)], sems.at[t]) for t in range(0, TT, 2)
    ]
    stores.append(pltpu.make_async_copy(drop_ref, drop_hbm, sems.at[TT]))
    images = []
    for t in range(TT):
        images.append(dot_nn(carried_ref[t], spatial_ref[t]))
        image_ref[t] = images[t]
        if t % 2:
            stores[t // 2].start()
    for t in range(TT):
        product = (probes_ref[t].astype(F32) * images[t]).reshape(WEEKS, PROBES, CELLS)
        drop_ref[t] = jnp.sum(product, axis=1) * (1.0 / PROBES)
    stores[-1].start()
    for store in stores:
        store.wait()


def per_device(probes, spatial, rho, foot_tile, foot_week, footprint, sigma):
    ns, nc = lax.axis_size("snd"), lax.axis_size("cell")
    sound = foot_tile.shape[0]
    half = sound // 2
    hbm = pl.BlockSpec(memory_space=pltpu.HBM)
    vmem = pl.BlockSpec(memory_space=pltpu.VMEM)
    one = pltpu.SemaphoreType.DMA
    dma = lambda n: pltpu.SemaphoreType.DMA((n,))
    operands = (
        probes.reshape(TT, WEEKS * PROBES, CELLS),
        spatial,
        rho,
        foot_tile.T,
        foot_week.T,
        footprint.reshape(sound * 4, CELLS),
        sigma.reshape(sound // 128, 128),
    )
    carried = pl.pallas_call(
        functools.partial(kernel, ns, nc, sound),
        out_shape=jax.ShapeDtypeStruct((TT, WEEKS * PROBES, CELLS), BF),
        in_specs=[hbm] * 7,
        out_specs=vmem,
        scratch_shapes=[
            pltpu.VMEM((TT, WEEKS * PROBES, CELLS), BF),
            pltpu.VMEM((TT, CELLS, CELLS), BF),
            pltpu.SMEM((TT,), F32),
            pltpu.VMEM((4, sound), jnp.int32),
            pltpu.VMEM((4, sound), jnp.int32),
            pltpu.VMEM((sound * 4, CELLS), BF),
            pltpu.VMEM((sound // 128, 128), F32),
            pltpu.VMEM((ns * TT, sound), F32),
            pltpu.VMEM((ns * TT, 128), F32),
            pltpu.VMEM((sound // 128, ns * 16, 512), BF),
            pltpu.VMEM((ns * SLOTS, sound), BF),
            pltpu.VMEM((sound, ns * SLOTS), BF),
            pltpu.VMEM((TT // SIDE, WEEKS * PROBES, SIDE * CELLS), BF),
            pltpu.VMEM((ns * SLOTS, SIDE * CELLS), BF),
            pltpu.VMEM((ns, SLOTS, CELLS), BF),
            pltpu.VMEM((ns, SLOTS, CELLS), BF),
            pltpu.VMEM((ns, 1, 128), F32),
            pltpu.VMEM((ns, 1, 128), F32),
            pltpu.VMEM((ns, 16, 128), BF),
            pltpu.VMEM((ns, 16, 128), BF),
            pltpu.VMEM((ns, 16, 128), BF),
            pltpu.VMEM((ns, 16, 128), BF),
            pltpu.VMEM((2, PROBES, half), F32),
            pltpu.VMEM((PROBES, half), F32),
            pltpu.VMEM((PROBES, half), BF),
            pltpu.VMEM((nc // 2, PROBES, half), BF),
            pltpu.VMEM((2, PROBES, half), BF),
            dma(7),
            one, one, one, one, one, one, one, one,
            one, one, dma(max(2, nc // 2)), dma(nc // 2), one, one,
        ],
        compiler_params=pltpu.CompilerParams(
            collective_id=0, has_side_effects=True, vmem_limit_bytes=40 * 1024 * 1024
        ),
    )(*(pltpu.with_memory_space_constraint(x, pltpu.HBM) for x in operands))
    image, drop = pl.pallas_call(
        finish,
        out_shape=(
            jax.ShapeDtypeStruct((TT, WEEKS * PROBES, CELLS), F32),
            jax.ShapeDtypeStruct((TT, WEEKS, CELLS), F32),
        ),
        in_specs=[vmem] * 3,
        out_specs=(hbm, hbm),
        scratch_shapes=[
            pltpu.VMEM((TT, WEEKS * PROBES, CELLS), F32),
            pltpu.VMEM((TT, WEEKS, CELLS), F32),
            dma(TT + 1),
        ],
        compiler_params=pltpu.CompilerParams(vmem_limit_bytes=4 * 1024 * 1024),
    )(carried, spatial, probes.reshape(TT, WEEKS * PROBES, CELLS))
    return image.reshape(TT, WEEKS, PROBES, CELLS), drop


def solution(mesh):
    placed = (
        P(("snd", "cell"), None, None, None),
        P(("snd", "cell"), None, None),
        P(("snd", "cell")),
        P("snd", None),
        P("snd", None),
        P("snd", None, None),
        P("snd"),
    )
    return jax.shard_map(
        per_device,
        mesh=mesh,
        in_specs=placed,
        out_specs=(P(("snd", "cell"), None, None, None), P(("snd", "cell"), None, None)),
        check_vma=False,
    )
```

```python
import functools

import jax
import jax.numpy as jnp
from jax import lax
from jax.experimental import pallas as pl
from jax.experimental.pallas import tpu as pltpu
from jax.sharding import PartitionSpec as P

BF = jnp.bfloat16
F32 = jnp.float32
MESH = pl.DeviceIdType.MESH

TT = 8
SLOTS = 64
WEEKS = 4
PROBES = 32
CELLS = 128
SIDE = 2


def dot_nn(a, b):
    return lax.dot_general(a, b, (((1,), (0,)), ((), ())), preferred_element_type=F32)


def dot_nt(a, b):
    return lax.dot_general(a, b, (((1,), (1,)), ((), ())), preferred_element_type=F32)


def iota(shape, dim):
    return lax.broadcasted_iota(jnp.int32, shape, dim)


def low_half(rows):
    return iota((rows, 128), 1) < 64


def packed(values):
    low = low_half(16)
    rows = []
    for lanes in (slice(0, 128), slice(128, 256)):
        upper, lower = values[:16, lanes], values[16:, lanes]
        rows.append(jnp.where(low, upper, pltpu.roll(lower, 64, 1)))
        rows.append(jnp.where(low, pltpu.roll(upper, 64, 1), lower))
    return jnp.stack(rows).astype(BF)


def unpacked(block):
    low = low_half(16)
    wide = block.astype(F32)
    cols = []
    for even, odd in ((wide[0], wide[1]), (wide[2], wide[3])):
        upper = jnp.where(low, even, pltpu.roll(odd, 64, 1))
        lower = jnp.where(low, pltpu.roll(even, 64, 1), odd)
        cols.append(jnp.concatenate([upper, lower], axis=0))
    return jnp.concatenate(cols, axis=1)


def doubled(ranks):
    rows, cols = ranks.shape
    wide = ranks.reshape(rows // 8, 8, cols)
    return jnp.concatenate([wide, wide - 1.0], axis=1).reshape(2 * rows, cols).astype(BF)


def one_hot(*ranks):
    rows, cols = ranks[0].shape
    wide = [r.reshape(rows // 16, 16, cols) for r in ranks]
    one, zero = jnp.ones((), BF), jnp.zeros((), BF)
    rows_of = []
    for q in range(4):
        same = wide[0] == jnp.asarray(2 * q, BF)
        for r in wide[1:]:
            same = same | (r == jnp.asarray(2 * q, BF))
        rows_of.append(jnp.where(same, one, zero))
    return jnp.concatenate(rows_of, axis=1).reshape(4 * rows, cols)


def kernel(
    ns, nc, sound,
    probes_hbm, spatial_hbm, rho_hbm, tile_hbm, week_hbm, foot_hbm, sigma_hbm,
    carried_ref,
    probes_ref, spatial_ref, rho_ref, tile_ref, week_ref, foot_ref, sigma_ref, order_ref, early_ref, ranks_ref, hot_ref, turned_ref, field_ref, wide_ref,
    send_f, recv_f, send_k, recv_k, send_v, recv_v, send_p, recv_p,
    send_c, recv_c, send_y, recv_y, recv_w,
    load_sem, ss_f, rs_f, ss_k, rs_k, ss_v, rs_v, ss_p, rs_p, ss_c, rs_c, ss_y, rs_y, ss_w, rs_w,
):
    me = lax.axis_index("snd")
    mine = lax.axis_index("cell")
    core, row_y = lax.rem(mine, 2), lax.div(mine, 2)
    nj = ns * TT
    groups = ns // 4
    ny = nc // 2
    half = sound // 2
    mx, mz = lax.div(me, 4), lax.rem(me, 4)
    near = {1: [0], 2: [0, 1], 4: [0, 1, 3, 2]}[groups]
    far = near[::-1]
    far_z = [2, 1, 3, 0]

    loads = [
        pltpu.make_async_copy(src, dst, load_sem.at[i])
        for i, (src, dst) in enumerate(
            (
                (tile_hbm, tile_ref),
                (week_hbm, week_ref),
                (foot_hbm, foot_ref),
                (spatial_hbm, spatial_ref),
                (probes_hbm, probes_ref),
                (sigma_hbm, sigma_ref),
                (rho_hbm, rho_ref),
            )
        )
    ]
    for load in loads:
        load.start()

    barrier = pltpu.get_barrier_semaphore()

    def greet(snd, cell):
        pl.semaphore_signal(barrier, inc=1, device_id={"snd": snd, "cell": cell}, device_id_type=MESH)

    def group_x(dx):
        return lax.rem(mx + dx, groups)

    def partner(dx, dz):
        return group_x(dx) * 4 + lax.rem(mz + dz, 4)

    for dx in far:
        for dz in far_z:
            if (dx, dz) != (0, 0):
                greet(partner(dx, dz), mine)
    for dy in range(1, ny):
        greet(me, lax.rem(row_y + dy, ny) * 2 + core)
    greet(me, row_y * 2 + 1 - core)

    def to_snd(refs, dest):
        src, dst, ss, rs = refs
        return pltpu.make_async_remote_copy(
            src_ref=src.at[dest], dst_ref=dst.at[me], send_sem=ss, recv_sem=rs,
            device_id={"snd": dest, "cell": mine}, device_id_type=MESH,
        )

    of_f = (send_f, recv_f, ss_f, rs_f)
    of_k = (send_k, recv_k, ss_k, rs_k)
    of_v = (send_v, recv_v, ss_v, rs_v)
    of_p = (send_p, recv_p, ss_p, rs_p)

    def send_group(refs, dx):
        for dz in far_z:
            if (dx, dz) != (0, 0):
                to_snd(refs, partner(dx, dz)).start()
        if dx == 0:
            refs[1][me] = refs[0][me]

    def of_others(buffer, sem):
        pltpu.make_async_copy(buffer.at[pl.ds(0, ns - 1)], buffer.at[pl.ds(0, ns - 1)], sem).wait()

    def arrived(refs):
        of_others(refs[1], refs[3])

    def sent(refs):
        of_others(refs[0], refs[2])

    def group_rows(dx, size):
        return pl.ds(pl.multiple_of(group_x(dx) * 4 * size, 4 * size), 4 * size)

    def group_of(dx):
        return pl.ds(pl.multiple_of(group_x(dx) * 4, 4), 4)

    loads[0].wait()
    loads[1].wait()
    tiles = tile_ref[...]
    weeks = week_ref[...]
    shift = nc.bit_length() - 1
    width = min(256, sound // 2)
    row_j = iota((nj, width), 0)
    upper = jnp.where(iota((width, width), 0) < iota((width, width), 1), 1.0, 0.0).astype(BF)
    counts = jnp.concatenate([upper, jnp.ones((width, width), BF)], axis=1)
    spread_e = jnp.where(iota((128, 512), 0) == iota((128, 512), 1) >> 2, 1.0, 0.0).astype(BF)
    pick_k = (iota((WEEKS, 512), 1) & 3) == iota((WEEKS, 512), 0)
    row_e = iota((nj, 512), 0).astype(F32)

    matched = ((tiles >> 3) & (nc - 1)) == mine
    local = jnp.where(matched, ((tiles >> (3 + shift)) << 3) | (tiles & 7), -1)
    carry = jnp.zeros((nj, width), F32)
    bits = jnp.zeros((nj, width), F32)
    for b in range(sound // width):
        if 2 * width * b == sound:
            early_ref[...] = carry[:, :128]
        lanes = slice(width * b, width * b + width)
        named = jnp.zeros((nj, width), F32)
        week_of = jnp.zeros((nj, width), jnp.int32)
        for k in range(4):
            same = local[k : k + 1, lanes] == row_j
            named = jnp.where(same, 1.0, named)
            week_of = jnp.where(same, weeks[k : k + 1, lanes], week_of)
        counted = dot_nn(named.astype(BF), counts)
        place = counted[:, :width] + carry
        order = jnp.where(named > 0.0, place, -1.0)
        carry = carry + counted[:, width:]
        bits = bits + (week_of << (place.astype(jnp.int32) * 2)).astype(F32)
        order_ref[:, lanes] = order
        for part in range(width // 128):
            a = width // 128 * b + part
            here = slice(128 * a, 128 * a + 128)
            spread_rank = dot_nn(order[:, 128 * part : 128 * part + 128].astype(BF), spread_e)
            spread_tile = dot_nn(local[:, here].astype(F32).astype(BF), spread_e)
            tile_e = jnp.sum(jnp.where(pick_k, spread_tile, 0.0), axis=0, keepdims=True)
            ranks_ref[a] = doubled(jnp.where(tile_e == row_e, spread_rank, -1.0))

    bits = jnp.sum(bits, axis=1, keepdims=True).astype(jnp.int32)
    lane = iota((TT, 128), 1)
    for d in range(ns):
        word = jnp.broadcast_to(bits[TT * d : TT * d + TT], (TT, 128))
        week = (word >> (((lane & 63) >> 3) * 2)) & 3
        row = jnp.sum(jnp.where((lane & 7) == iota((TT, 128), 0), week.astype(F32), 0.0), axis=0, keepdims=True)
        send_k[d] = row

    loads[2].wait()

    both = jnp.concatenate([foot_ref[: 2 * sound, :], foot_ref[2 * sound :, :]], axis=1)
    pairs = sound // 256

    def pick_feet(dx):
        for part in range(2):
            first = group_x(dx) * 4 + 2 * part
            rows = pl.ds(pl.multiple_of(first * 16, 32), 32)
            picks = [one_hot(ranks_ref[a, rows, :], ranks_ref[a + pairs, rows, :]) for a in range(pairs)]
            found = dot_nn(jnp.concatenate(picks, axis=1), both).reshape(2, 8, TT, 2 * CELLS)
            early = early_ref[pl.ds(pl.multiple_of(first * TT, 16), 16), :].reshape(2, TT, CELLS)
            kept = [jnp.where(early > float(r), found[:, r, :, :CELLS], found[:, r, :, CELLS:]) for r in range(8)]
            send_f[pl.ds(first, 2)] = jnp.stack(kept, axis=1).reshape(2, SLOTS, CELLS).astype(BF)

    for dx in far[: groups // 2]:
        pick_feet(dx)
    if groups == 1:
        pick_feet(0)
    pl.semaphore_wait(barrier, ns - 1 + ny - 1 + 1)
    for dx in far:
        send_group(of_k, dx)
    for dx in far[: groups // 2]:
        send_group(of_f, dx)
    for dx in far[groups // 2 :]:
        if groups > 1:
            pick_feet(dx)
        send_group(of_f, dx)

    for b in range(sound // 256):
        lanes = slice(256 * b, 256 * b + 256)
        hot_ref[:, lanes] = one_hot(doubled(order_ref[:, lanes]))
        turned_ref[lanes, :] = hot_ref[:, lanes].T

    for load in loads[3:]:
        load.wait()
    for t in range(TT):
        spread = dot_nt(probes_ref[t], spatial_ref[t])
        lanes = slice(CELLS * (t % SIDE), CELLS * (t % SIDE) + CELLS)
        running = spread[:PROBES]
        field_ref[t // SIDE, :PROBES, lanes] = running.astype(BF)
        for w in range(1, WEEKS):
            running = spread[PROBES * w : PROBES * w + PROBES] + rho_ref[t] * running
            field_ref[t // SIDE, PROBES * w : PROBES * w + PROBES, lanes] = running.astype(BF)

    lane_side = (iota((PROBES, 256), 1) & 7) // SIDE
    row_tile = (iota((256, CELLS), 0) & (SIDE - 1)).astype(F32).astype(BF)
    fields = field_ref[...].reshape(TT // SIDE * WEEKS * PROBES, SIDE * CELLS)
    codes = {}
    arrived(of_f)
    arrived(of_k)
    for dx in near:
        names = recv_k[group_of(dx)]
        low = low_half(1)
        code = jnp.concatenate([jnp.where(low, names[0], names[1]), jnp.where(low, names[2], names[3])], axis=1)
        codes[dx] = jnp.broadcast_to(code, (PROBES, 256))
        feet = recv_f[group_of(dx)].reshape(256, CELLS)
        sides = [jnp.where(row_tile == jnp.asarray(h, BF), feet, jnp.zeros((), BF)) for h in range(SIDE)]
        wide = jnp.concatenate(sides, axis=1)
        wide_ref[group_rows(dx, SLOTS), :] = wide
        full = dot_nt(fields, wide)
        full = full.reshape(TT // SIDE, WEEKS, PROBES, 256)
        value = jnp.zeros((PROBES, 256), F32)
        for w in range(WEEKS):
            here = full[0, w]
            for g in range(1, TT // SIDE):
                here = jnp.where(lane_side == g, full[g, w], here)
            value = jnp.where(codes[dx] == float(w), here, value)
        send_v[group_of(dx)] = packed(value)
    for dx in far:
        send_group(of_v, dx)

    sent(of_f)
    sent(of_k)

    seen = jnp.zeros((PROBES, sound), F32)
    arrived(of_v)
    for dx in near:
        seen = seen + dot_nn(unpacked(recv_v[group_of(dx)]).astype(BF), hot_ref[group_rows(dx, SLOTS), :])
    send_c[0] = seen[:, :half]
    send_c[1] = seen[:, half:]
    other_core = {"snd": me, "cell": row_y * 2 + 1 - core}
    swap = pltpu.make_async_remote_copy(
        src_ref=send_c.at[1 - core], dst_ref=recv_c, send_sem=ss_c, recv_sem=rs_c,
        device_id=other_core, device_id_type=MESH,
    )
    swap.start()
    swap.wait_recv()
    total = send_c[core] + recv_c[...]
    send_y[...] = total.astype(BF)

    def over_y(dy, slot):
        return pltpu.make_async_remote_copy(
            src_ref=send_y, dst_ref=recv_y.at[slot], send_sem=ss_y.at[dy], recv_sem=rs_y,
            device_id={"snd": me, "cell": lax.rem(row_y + dy, ny) * 2 + core}, device_id_type=MESH,
        )

    steps_y = {1: [], 2: [1], 4: [2, 1, 3]}[ny]
    for dy in steps_y:
        over_y(dy, row_y).start()
    sent(of_v)
    swap.wait_send()
    if ny > 1:
        pltpu.make_async_copy(recv_y.at[pl.ds(0, ny - 1)], recv_y.at[pl.ds(0, ny - 1)], rs_y).wait()
    for dy in reversed(steps_y):
        total = total + recv_y[lax.rem(row_y + dy, ny)].astype(F32)
    own = half // 128
    sigma = jnp.concatenate([sigma_ref[pl.ds(core * own + i, 1), :] for i in range(own)], axis=1)
    recv_w[core] = (total / (sigma * sigma)).astype(BF)
    share = pltpu.make_async_remote_copy(
        src_ref=recv_w.at[core], dst_ref=recv_w.at[core], send_sem=ss_w, recv_sem=rs_w,
        device_id=other_core, device_id_type=MESH,
    )
    share.start()
    share.wait_recv()

    weighted = jnp.concatenate([recv_w[0], recv_w[1]], axis=1)
    backs = dot_nn(weighted, turned_ref[...])
    for x in range(groups):
        send_p[4 * x : 4 * x + 4] = packed(backs[:, 256 * x : 256 * x + 256])
    for dx in far:
        send_group(of_p, dx)

    for dy in steps_y:
        over_y(dy, row_y).wait_send()

    at_side = [lane_side.astype(F32).astype(BF) == jnp.asarray(g, BF) for g in range(TT // SIDE)]
    arrived(of_p)
    spread = []
    for dx in near:
        value, code = unpacked(recv_p[group_of(dx)]).astype(BF), codes[dx].astype(BF)
        by_week = [jnp.where(code == jnp.asarray(w, BF), value, jnp.zeros((), BF)) for w in range(WEEKS)]
        spread.append([[jnp.where(at, part, jnp.zeros((), BF)) for part in by_week] for at in at_side])
    feet = jnp.concatenate([wide_ref[group_rows(dx, SLOTS), :] for dx in near], axis=0)
    for g in range(TT // SIDE):
        kept = jnp.concatenate([jnp.concatenate(parts[g], axis=0) for parts in spread], axis=1)
        adjoint = dot_nn(kept, feet)
        for h in range(SIDE):
            here = adjoint[:, CELLS * h : CELLS * h + CELLS]
            running = here[PROBES * (WEEKS - 1) :]
            carried = [running]
            for w in range(WEEKS - 2, -1, -1):
                running = here[PROBES * w : PROBES * w + PROBES] + rho_ref[SIDE * g + h] * running
                carried.append(running)
            carried_ref[SIDE * g + h] = jnp.concatenate(carried[::-1], axis=0).astype(BF)

    sent(of_p)
    share.wait_send()


def finish(carried_ref, spatial_ref, probes_ref, image_hbm, drop_hbm, image_ref, drop_ref, sems):
    stores = [
        pltpu.make_async_copy(image_ref.at[pl.ds(t, 2)], image_hbm.at[pl.ds(t, 2)], sems.at[t]) for t in range(0, TT, 2)
    ]
    stores.append(pltpu.make_async_copy(drop_ref, drop_hbm, sems.at[TT]))
    images = []
    for t in range(TT):
        images.append(dot_nn(carried_ref[t], spatial_ref[t]))
        image_ref[t] = images[t]
        if t % 2:
            stores[t // 2].start()
    for t in range(TT):
        product = (probes_ref[t].astype(F32) * images[t]).reshape(WEEKS, PROBES, CELLS)
        drop_ref[t] = jnp.sum(product, axis=1) * (1.0 / PROBES)
    stores[-1].start()
    for store in stores:
        store.wait()


def per_device(probes, spatial, rho, foot_tile, foot_week, footprint, sigma):
    ns, nc = lax.axis_size("snd"), lax.axis_size("cell")
    sound = foot_tile.shape[0]
    half = sound // 2
    hbm = pl.BlockSpec(memory_space=pltpu.HBM)
    vmem = pl.BlockSpec(memory_space=pltpu.VMEM)
    one = pltpu.SemaphoreType.DMA
    dma = lambda n: pltpu.SemaphoreType.DMA((n,))
    operands = (
        probes.reshape(TT, WEEKS * PROBES, CELLS),
        spatial,
        rho,
        foot_tile.T,
        foot_week.T,
        footprint.reshape(sound * 4, CELLS),
        sigma.reshape(sound // 128, 128),
    )
    carried = pl.pallas_call(
        functools.partial(kernel, ns, nc, sound),
        out_shape=jax.ShapeDtypeStruct((TT, WEEKS * PROBES, CELLS), BF),
        in_specs=[hbm] * 7,
        out_specs=vmem,
        scratch_shapes=[
            pltpu.VMEM((TT, WEEKS * PROBES, CELLS), BF),
            pltpu.VMEM((TT, CELLS, CELLS), BF),
            pltpu.SMEM((TT,), F32),
            pltpu.VMEM((4, sound), jnp.int32),
            pltpu.VMEM((4, sound), jnp.int32),
            pltpu.VMEM((sound * 4, CELLS), BF),
            pltpu.VMEM((sound // 128, 128), F32),
            pltpu.VMEM((ns * TT, sound), F32),
            pltpu.VMEM((ns * TT, 128), F32),
            pltpu.VMEM((sound // 128, ns * 16, 512), BF),
            pltpu.VMEM((ns * SLOTS, sound), BF),
            pltpu.VMEM((sound, ns * SLOTS), BF),
            pltpu.VMEM((TT // SIDE, WEEKS * PROBES, SIDE * CELLS), BF),
            pltpu.VMEM((ns * SLOTS, SIDE * CELLS), BF),
            pltpu.VMEM((ns, SLOTS, CELLS), BF),
            pltpu.VMEM((ns, SLOTS, CELLS), BF),
            pltpu.VMEM((ns, 1, 128), F32),
            pltpu.VMEM((ns, 1, 128), F32),
            pltpu.VMEM((ns, 16, 128), BF),
            pltpu.VMEM((ns, 16, 128), BF),
            pltpu.VMEM((ns, 16, 128), BF),
            pltpu.VMEM((ns, 16, 128), BF),
            pltpu.VMEM((2, PROBES, half), F32),
            pltpu.VMEM((PROBES, half), F32),
            pltpu.VMEM((PROBES, half), BF),
            pltpu.VMEM((nc // 2, PROBES, half), BF),
            pltpu.VMEM((2, PROBES, half), BF),
            dma(7),
            one, one, one, one, one, one, one, one,
            one, one, dma(max(2, nc // 2)), one, one, one,
        ],
        compiler_params=pltpu.CompilerParams(
            collective_id=0, has_side_effects=True, vmem_limit_bytes=40 * 1024 * 1024
        ),
    )(*(pltpu.with_memory_space_constraint(x, pltpu.HBM) for x in operands))
    image, drop = pl.pallas_call(
        finish,
        out_shape=(
            jax.ShapeDtypeStruct((TT, WEEKS * PROBES, CELLS), F32),
            jax.ShapeDtypeStruct((TT, WEEKS, CELLS), F32),
        ),
        in_specs=[vmem] * 3,
        out_specs=(hbm, hbm),
        scratch_shapes=[
            pltpu.VMEM((TT, WEEKS * PROBES, CELLS), F32),
            pltpu.VMEM((TT, WEEKS, CELLS), F32),
            dma(TT + 1),
        ],
        compiler_params=pltpu.CompilerParams(vmem_limit_bytes=4 * 1024 * 1024),
    )(carried, spatial, probes.reshape(TT, WEEKS * PROBES, CELLS))
    return image.reshape(TT, WEEKS, PROBES, CELLS), drop


def solution(mesh):
    placed = (
        P(("snd", "cell"), None, None, None),
        P(("snd", "cell"), None, None),
        P(("snd", "cell")),
        P("snd", None),
        P("snd", None),
        P("snd", None, None),
        P("snd"),
    )
    return jax.shard_map(
        per_device,
        mesh=mesh,
        in_specs=placed,
        out_specs=(P(("snd", "cell"), None, None, None), P(("snd", "cell"), None, None)),
        check_vma=False,
    )
```
